32 devices in a mesh: groups: 2 (over x), gy: 16 (over z, y, core).
Axes of the slice: x: 2, y: 2, z: 4, core: 2. Of those that a mesh axis runs over, the one named last changes fastest.
Arguments:
- tiles: bfloat16 [1024, 16, 128], P(('groups', 'gy')), parts along dimension 0, may hold values from -6 to 6
- entry_dest: int32 [1024, 1], P('groups'), parts along dimension 0, may hold values from 0 to 15; in each aligned block of 32 rows (0 to 31, 32 to 63, ...) at most 4 rows name the same one
- entry_tile: int32 [1024], P('groups'), parts along dimension 0, may hold values from 0 to 31
- entry_z: int32 [1024], P('groups'), parts along dimension 0, may hold values from 0 to 3
- entry_xb: int32 [1024], P('groups'), parts along dimension 0, may hold values from 0 to 3
- entry_ky: int32 [1024], P('groups'), parts along dimension 0, may hold values from 0 to 7
- entry_kx: int32 [1024], P('groups'), parts along dimension 0, may hold values from 0 to 7
- wy_table: bfloat16 [8, 8, 16], replicated, may hold values from 0 to 1
- wx_table: bfloat16 [8, 128, 128], replicated, may hold values from 0 to 1
- w_first: bfloat16 [32, 1, 3, 3, 3], replicated, may hold values from -1.25 to 1.25
- b_first: float32 [32], replicated, may hold values from -1.5 to 1.5
- w_second: bfloat16 [32, 32, 3, 3, 3], replicated, may hold values from -0.21875 to 0.21875
- b_second: float32 [32], replicated, may hold values from -1.5 to 1.5
- w_third: bfloat16 [32, 32, 3, 3, 3], replicated, may hold values from -0.21875 to 0.21875
- b_third: float32 [32], replicated, may hold values from -1.5 to 1.5
Outputs:
- affinity_features: bfloat16 [32, 8, 128, 512], P(None, 'groups', 'gy'), parts along dimension 1
The draws below stay inside these ranges and needn't reach their ends.
There are 2 independent parts, one for each index of `groups`. The reference program is written for one: setup_inputs(seed, part) draws one part's arguments, and reference() takes and returns one part's arrays. A program takes and returns all parts, laid end to end along the dimension named above; an argument that names none is the same for every part. Nothing has to cross between parts.
Inputs may be any that keep to these rules, and one draw needn't show every extreme that they name: `entry_dest`: rows 32 * s to 32 * s + 31 are the entries of the tiles of device s of gy; among one device's rows no brick is named more than 4 times, a bound that some block reaches.
All inputs are finite; a program needn't handle non-finite values.
Results may differ from the reference program's by a relative error of at most 0.0064.
Values may be sent and summed in bfloat16 or wider, within the bound.
No kernel may reach another device: no remote copies, remote signals or barrier semaphores. Data moves between devices by JAX's collectives and lax.ppermute only.
A program may use at most 64 MiB of HBM per device.

```python
import math
import jax
import jax.numpy as jnp
import numpy as np
from jax import lax

C = 32
X = 512
YB = 8
Z = 4
SH = 16
SW = 128
TILES_DEV = 32
CAP = 4
KY = 8
KX = 8
E_DEV = 32
ENTRIES = 512
N_GY = 16


def draw_wy_table(key, part):
    fraction = jax.random.uniform(key, (KY, YB, 1), jnp.float32)
    out_row = lax.broadcasted_iota(jnp.int32, (KY, YB, SH), 1)
    source_row = lax.broadcasted_iota(jnp.int32, (KY, YB, SH), 2)
    lower_row = out_row * SH // YB
    upper_row = jnp.minimum(lower_row + 1, SH - 1)
    low_weight = jnp.where(source_row == lower_row, 1.0 - fraction, 0.0)
    high_weight = jnp.where(source_row == upper_row, fraction, 0.0)
    return (low_weight + high_weight).astype(jnp.bfloat16)


def draw_wx_table(key, part):
    fraction = jax.random.uniform(key, (KX, 1, SW), jnp.float32)
    source_col = lax.broadcasted_iota(jnp.int32, (KX, SW, SW), 1)
    output_col = lax.broadcasted_iota(jnp.int32, (KX, SW, SW), 2)
    upper_col = jnp.minimum(output_col + 1, SW - 1)
    low_weight = jnp.where(source_col == output_col, 1.0 - fraction, 0.0)
    high_weight = jnp.where(source_col == upper_col, fraction, 0.0)
    return (low_weight + high_weight).astype(jnp.bfloat16)


def with_ends(drawn, key, smallest, top_value):
    shape = drawn.shape
    place = [jax.random.randint(jax.random.fold_in(key, axis), (), 0, shape[axis]) for axis in range(len(shape))]
    drawn = drawn.at[tuple(place)].set(smallest)
    longest = shape.index(max(shape))
    place[longest] = (place[longest] + 1) % shape[longest]
    return drawn.at[tuple(place)].set(top_value)


def block_scale(stream_key, dims, pieces, low, top_value):
    factor_of, own = 1.0, jax.random.fold_in(stream_key, 6)
    for axis_at, shards_of in pieces:
        steps = jnp.exp(jax.random.uniform(jax.random.fold_in(own, axis_at), (shards_of,), jnp.float32, low / len(pieces), top_value / len(pieces)))
        factor_of = factor_of * jnp.repeat(steps, dims[axis_at] // shards_of).reshape([-1 if axis == axis_at else 1 for axis in range(len(dims))])
    return factor_of


def assign_block(rng, own, number, rows, count, top, most, slope):
    ranking = jax.random.permutation(rng, count)
    crowded, usual = shares(count, rows * top, most, slope, True), shares(count, rows * top, most, slope, False)
    places = jnp.arange(count)

    def named(tallies, turn):
        used = int((tallies > 0).sum())
        fixed = max(1, used // 4)
        passed = fixed + (places - fixed + turn * (used - fixed)) % max(1, count - fixed)
        return jnp.zeros((count,), jnp.int32).at[ranking[jnp.where(places < fixed, places, passed)]].set(jnp.asarray(tallies, jnp.int32))

    tallies = jnp.where(number % 4 == 0, named(crowded, number // 4), named(usual, number - number // 4 - 1))
    mixed = jax.random.permutation(jax.random.fold_in(own, 3), count)
    donor, receiver = mixed[0:count // 2 * 2:2], mixed[1:count // 2 * 2:2]
    slack = jnp.minimum(tallies[donor] - 1, most - tallies[receiver]) // 2
    slack = jnp.where((donor == ranking[0]) | (receiver == ranking[0]) | (tallies[receiver] == 0), 0, jnp.maximum(slack, 0))
    passed = jax.random.randint(jax.random.fold_in(own, 4), (count // 2,), 0, 1 << 20) % (slack + 1)
    tallies = tallies.at[donor].add(-passed).at[receiver].add(passed)
    members = jnp.searchsorted(jnp.cumsum(tallies), jnp.arange(rows * top), side="right").astype(jnp.int32)
    listing = members.reshape(top, rows).T
    listing = listing[jax.random.permutation(jax.random.fold_in(own, 1), rows)]
    turn = jax.random.randint(jax.random.fold_in(own, 2), (rows, 1), 0, top)
    return jnp.take_along_axis(listing, (jnp.arange(top)[None, :] + turn) % top, axis=1)


def shares(count, total, most, slope, full):
    loads = [(1 << 20) // math.isqrt(standing ** slope) + 1 for standing in range(1, count + 1)]
    largest = most if full else min(most, max(-(-total // count), total * loads[0] // sum(loads)))
    least = 1 if total - largest >= count - 1 else 0
    counts, surplus = [largest] + [least] * (count - 1), total - largest - least * (count - 1)
    while surplus > 0:
        candidates = [i for i in range(1, count) if counts[i] < largest] or [i for i in range(1, count) if counts[i] < most]
        mass, left = sum([loads[i] for i in candidates]), surplus
        for i in candidates:
            addition = min(most - counts[i], max(1, left * loads[i] // mass), surplus)
            counts[i] = counts[i] + addition
            surplus = surplus - addition
    return np.array(counts)


def centred(key, shape, scale, most, shards=(), kind=jnp.bfloat16):
    drawn = jax.random.normal(key, shape, jnp.float32) * scale
    if len(shards) > 0:
        drawn = block_scale(key, shape, shards, -0.22, 0.18) * drawn
    return jnp.clip(drawn, min=-most, max=most).astype(kind)


def setup_inputs(seed: int = 0, part: int = 0) -> dict:
    keys = jax.random.split(jax.random.key(seed), 16)
    part_keys = jax.random.split(jax.random.fold_in(keys[15], part), 16)
    tiles = centred(part_keys[0], (N_GY * TILES_DEV, SH, SW), 1.0, 6.0, ((0, 16),))
    entry_dest_keys = jax.random.split(jax.random.fold_in(part_keys[1], 1), ENTRIES // E_DEV)
    entry_dest_turns = jax.random.permutation(jax.random.fold_in(part_keys[1], 3), ENTRIES // E_DEV)
    entry_dest = jax.vmap(lambda own, number: assign_block(jax.random.fold_in(part_keys[1], 2), own, number, E_DEV, N_GY, 1, CAP, 2))(entry_dest_keys, entry_dest_turns).reshape((ENTRIES, 1))
    entry_tile = with_ends(jax.random.randint(part_keys[2], (ENTRIES,), 0, TILES_DEV), jax.random.fold_in(part_keys[2], 1), 0, TILES_DEV - 1).astype(jnp.int32)
    entry_z = with_ends(jax.random.randint(part_keys[3], (ENTRIES,), 0, Z), jax.random.fold_in(part_keys[3], 1), 0, Z - 1).astype(jnp.int32)
    entry_xb = with_ends(jax.random.randint(part_keys[4], (ENTRIES,), 0, X // SW), jax.random.fold_in(part_keys[4], 1), 0, (X // SW) - 1).astype(jnp.int32)
    entry_ky = with_ends(jax.random.randint(part_keys[5], (ENTRIES,), 0, KY), jax.random.fold_in(part_keys[5], 1), 0, KY - 1).astype(jnp.int32)
    entry_kx = with_ends(jax.random.randint(part_keys[6], (ENTRIES,), 0, KX), jax.random.fold_in(part_keys[6], 1), 0, KX - 1).astype(jnp.int32)
    wy_table = draw_wy_table(jax.random.fold_in(keys[15], 71), part)
    wx_table = draw_wx_table(jax.random.fold_in(keys[15], 71), part)
    w_first = centred(keys[9], (C, 1, 3, 3, 3), 27 ** -0.5, 1.25)
    b_first = centred(keys[10], (C,), 0.3, 1.5, (), jnp.float32)
    w_second = centred(keys[11], (C, C, 3, 3, 3), (27 * C) ** -0.5, 0.21875)
    b_second = centred(keys[12], (C,), 0.3, 1.5, (), jnp.float32)
    w_third = centred(keys[13], (C, C, 3, 3, 3), (27 * C) ** -0.5, 0.21875)
    b_third = centred(keys[14], (C,), 0.3, 1.5, (), jnp.float32)
    return dict(tiles=tiles, entry_dest=entry_dest, entry_tile=entry_tile, entry_z=entry_z, entry_xb=entry_xb, entry_ky=entry_ky, entry_kx=entry_kx, wy_table=wy_table, wx_table=wx_table, w_first=w_first, b_first=b_first, w_second=w_second, b_second=b_second, w_third=w_third, b_third=b_third)


def conv_layer(features, weight, bias):
    result = lax.conv_general_dilated(
        features[None].astype(jnp.float32), weight.astype(jnp.float32), (1, 1, 1),
        ((1, 1), (1, 1), (1, 1)), dimension_numbers=("NCDHW", "OIDHW", "NCDHW"),
        precision=lax.Precision.HIGHEST)[0]
    return jax.nn.relu(result + bias[:, None, None, None]).astype(jnp.bfloat16)


def reference(tiles, entry_dest, entry_tile, entry_z, entry_xb, entry_ky, entry_kx, wy_table, wx_table, w_first, b_first, w_second, b_second, w_third, b_third):
    target_brick = entry_dest[:, 0]
    count = target_brick.shape[0]
    per_device = count // N_GY
    source = (jnp.arange(count, dtype=jnp.int32) // per_device).astype(jnp.int32)
    picked = tiles[(source * TILES_DEV + entry_tile).astype(jnp.int32)].astype(jnp.float32)
    vertical = wy_table[entry_ky].astype(jnp.float32)
    row_samples = jnp.einsum("eys,esw->eyw", vertical, picked).astype(jnp.bfloat16)
    flat_rows = row_samples.reshape(count * YB, SW)
    patches = jnp.zeros((count, YB, SW), jnp.float32)
    for block_index in range(KX):
        product = jnp.dot(flat_rows, wx_table[block_index], preferred_element_type=jnp.float32).reshape(count, YB, SW)
        patches = patches + jnp.where((entry_kx == block_index)[:, None, None], product, jnp.zeros_like(product))
    rendered = jnp.zeros((Z, N_GY, YB, X // SW, SW), jnp.float32)
    rendered = rendered.at[entry_z, target_brick, :, entry_xb, :].add(patches)
    image = rendered.reshape(Z, N_GY * YB, X).astype(jnp.bfloat16)
    first = conv_layer(image[None], w_first, b_first)
    second = conv_layer(first, w_second, b_second)
    return conv_layer(second, w_third, b_third)
```

```python
import functools

import jax
import jax.numpy as jnp
from jax import lax
from jax.experimental import pallas as pl
from jax.experimental.pallas import tpu as pltpu
from jax.sharding import PartitionSpec as P

X = 512
YB = 8
Z = 4
CAP = 4
C = 32
HALO = 3
YW = 16
ROWS = YW * CAP
LANES = 128
F32 = jnp.float32
BF16 = jnp.bfloat16


def iota(shape, dim):
    return lax.broadcasted_iota(jnp.int32, shape, dim)


def send_kernel(per, axis, dest_ref, tile_ref, ky_ref, kx_ref, tiles_ref, wy_ref, wx_ref, out_ref, wyt, count):
    bricks = count.shape[0]
    base = lax.axis_index(axis) * per
    sh = wy_ref.shape[1]
    kys, kxs = wy_ref.shape[0] // YB, wx_ref.shape[0] // LANES
    cols = tiles_ref.shape[0]
    spread = (iota((sh, cols), 0) == iota((sh, cols), 1) % sh).astype(BF16)
    wyt[...] = jnp.dot(wy_ref[...], spread, preferred_element_type=F32).reshape(kys, YB, cols)

    def clear(i, carry):
        count[i] = 0
        return carry

    lax.fori_loop(0, bricks, clear, 0)
    tile_of_col = iota((YB, cols), 1) // sh
    entry_of_lane = iota((YB, per * YB), 1) // YB
    key = jnp.zeros((YB, per * YB), jnp.int32)
    vertical, kinds = [], []
    for e in range(per):
        dest = dest_ref[0, base + e]
        rank = count[dest]
        count[dest] = rank + 1
        key = jnp.where(entry_of_lane == e, dest * (YB * CAP) + rank, key)
        vertical.append(jnp.where(tile_of_col == tile_ref[0, base + e], wyt[ky_ref[0, base + e]], 0.0))
        kinds.append(kx_ref[0, base + e])
    key = (key + CAP * (iota((YB, per * YB), 1) % YB))[:1]
    samples = jnp.dot(jnp.concatenate(vertical, axis=0).astype(BF16), tiles_ref[...], preferred_element_type=F32)
    samples = samples.astype(BF16).astype(F32)
    by_kind = []
    for k in range(kxs):
        by_kind.append(
            jnp.concatenate(
                [jnp.where(kinds[e] == k, samples[e * YB : (e + 1) * YB], 0.0) for e in range(per)], axis=0
            ).astype(BF16)
        )
    patches = jnp.dot(jnp.concatenate(by_kind, axis=1), wx_ref[...], preferred_element_type=F32).astype(BF16)
    block = 256
    for j in range(bricks * ROWS // block):
        row = j * block + iota((block, per * YB), 0)
        row_key = (row // ROWS) * (YB * CAP) + row % ROWS - HALO * CAP
        chooser = (row_key == key).astype(F32).astype(BF16)
        out_ref[j * block : (j + 1) * block] = jnp.dot(chooser, patches, preferred_element_type=F32).astype(BF16)


def banded(w_ref, out_ref):
    wide = Z * C
    lane = iota((C, wide), 1)
    zero = jnp.zeros((wide, wide), BF16)
    gap = jnp.zeros((C, wide - 3 * C), F32)
    for c in range(3):
        for b in range(3):
            taps = [w_ref[(a * 3 + b) * 3 + c].astype(F32) for a in range(3)]
            row = jnp.concatenate(taps + [gap], axis=1)
            rows = []
            for z in range(Z):
                moved = row if z == 1 else pltpu.roll(row, ((z - 1) * C) % wide, 1)
                if z == 0:
                    moved = jnp.where(lane < 2 * C, moved, 0.0)
                if z == Z - 1:
                    moved = jnp.where(lane >= (Z - 2) * C, moved, 0.0)
                rows.append(moved)
            block = jnp.concatenate(rows, axis=0).astype(BF16)
            for y in range(2):
                out_ref[c, y * wide : (y + 1) * wide, (y + b) * wide : (y + b + 1) * wide] = block
        out_ref[c, :wide, 3 * wide :] = zero
        out_ref[c, wide:, :wide] = zero


def bias_rows(b_ref):
    column = jnp.sum(
        jnp.where(iota((C, C), 0) == iota((C, C), 1), jnp.broadcast_to(b_ref[...], (C, C)), 0.0), axis=1, keepdims=True
    )
    return jnp.concatenate([jnp.broadcast_to(column, (C, LANES))] * Z, axis=0)


def prep_kernel(per, axis, dest_ref, z_ref, xb_ref, w1_ref, b1_ref, w2_ref, b2_ref, w3_ref, b3_ref,
                place_ref, m1_ref, m2_ref, m3_ref, bias_ref, taps):
    own = lax.axis_index(axis)
    banded(w2_ref, m2_ref)
    banded(w3_ref, m3_ref)
    for n, b_ref in enumerate((b1_ref, b2_ref, b3_ref)):
        bias_ref[n] = bias_rows(b_ref)
    taps[...] = jnp.zeros_like(taps)
    for ab in range(9):
        taps[ab * 4 : ab * 4 + 3, :C] = w1_ref[ab].astype(F32)
    first = jnp.transpose(taps[...])[:C].astype(BF16)
    wide1 = m1_ref.shape[1]
    t = iota((LANES, wide1), 0)
    col = iota((LANES, wide1), 1)
    t_c, t_b, t_a = t % 4, (t // 4) % 3, t // 12
    for y in range(2):
        for z in range(Z):
            z_in = z + t_a - 1
            good = (t < 36) & (t_c < 3) & (z_in >= 0) & (z_in < Z)
            pick = (good & (col == t_c * (4 * Z) + (t_b + y) * Z + z_in)).astype(F32).astype(BF16)
            at = (y * Z + z) * C
            m1_ref[at : at + C, :] = jnp.dot(first, pick, preferred_element_type=F32).astype(BF16)
    chunks, rows, wide = place_ref.shape
    earlier = (
        (iota((LANES, LANES), 0) < iota((LANES, LANES), 1))
        & (iota((LANES, LANES), 0) // per == iota((LANES, LANES), 1) // per)
    ).astype(F32).astype(BF16)
    slot_k, y_k, src_k = iota((wide, LANES), 0) % CAP, (iota((wide, LANES), 0) // CAP) % YW, iota((wide, LANES), 0) // ROWS
    same_source = src_k == iota((wide, LANES), 1) // per
    code_row = (iota((rows, LANES), 0) // ROWS) * Z + iota((rows, LANES), 0) % Z
    same_y = (iota((rows, wide), 0) // Z) % YW == (iota((rows, wide), 1) // CAP) % YW

    def one(n, carry):
        at = pl.multiple_of(n * LANES, LANES)
        dest = jnp.broadcast_to(dest_ref[:, pl.ds(at, LANES)], (8, LANES))
        code = xb_ref[:, pl.ds(at, LANES)] * Z + z_ref[:, pl.ds(at, LANES)]
        sub = iota((8, LANES), 0)
        named = (dest == own - 1 + sub) & (sub < 3)
        rank = jnp.dot(named.astype(F32).astype(BF16), earlier, preferred_element_type=F32).astype(jnp.int32)
        slot = jnp.where(named, rank, -1)
        wanted = jnp.where(y_k < HALO, slot[0:1], jnp.where(y_k < HALO + YB, slot[1:2], slot[2:3]))
        held = (same_source & (slot_k == wanted) & (y_k < YB + 2 * HALO)).astype(F32).astype(BF16)
        cell = (code_row == code).astype(F32).astype(BF16)
        hits = lax.dot_general(cell, held, (((1,), (1,)), ((), ())), preferred_element_type=F32)
        place_ref[n] = jnp.where(same_y, hits, 0.0).astype(BF16)
        return carry

    if chunks <= 8:
        for n in range(chunks):
            one(n, 0)
    else:
        lax.fori_loop(0, chunks, one, 0)


def shifted(values):
    lane = iota(values.shape, 1)
    last = values.shape[1] - 1
    return (
        jnp.where(lane == 0, 0.0, pltpu.roll(values, 1, 1)),
        values,
        jnp.where(lane == last, 0.0, pltpu.roll(values, last, 1)),
    )


def conv_kernel(axis, bricks, arrived_ref, place_ref, m1_ref, m2_ref, m3_ref, bias_ref, out_ref, g2, g3, staged):
    own = lax.axis_index(axis)
    above, below = (own > 0).astype(F32), (own < bricks - 1).astype(F32)
    chunks, rows, wide = place_ref.shape
    wide_m = Z * C

    def place(n, total):
        at = n * wide if isinstance(n, int) else pl.multiple_of(n * wide, wide)
        return total + jnp.dot(place_ref[n], arrived_ref[pl.ds(at, wide)], preferred_element_type=F32)

    total = jnp.zeros((rows, LANES), F32)
    if chunks <= 8:
        for n in range(chunks):
            total = place(n, total)
    else:
        total = lax.fori_loop(0, chunks, place, total)
    image = jnp.concatenate([total[n * ROWS : (n + 1) * ROWS] for n in range(X // LANES)], axis=1)
    image = image.astype(BF16).astype(F32)
    moved = shifted(image)

    def bias_of(n):
        return jnp.concatenate([bias_ref[n]] * (X // LANES), axis=1)

    pairs1, pairs2, pairs3 = YB // 2 + 2, YB // 2 + 1, YB // 2
    for p in range(pairs1):
        gathered = jnp.concatenate([m[2 * p * Z : (2 * p + 4) * Z] for m in moved], axis=0)
        gathered = jnp.concatenate([gathered, jnp.zeros((m1_ref.shape[1] - 12 * Z, X), F32)], axis=0).astype(BF16)
        acc = jnp.dot(m1_ref[...], gathered, preferred_element_type=F32)
        for y in range(2):
            value = jnp.maximum(acc[y * wide_m : (y + 1) * wide_m] + bias_of(0), 0.0)
            if p == 0:
                value = value * above
            if p == pairs1 - 1:
                value = value * below
            for c, v in enumerate(shifted(value)):
                g2[c, (2 * p + y) * wide_m : (2 * p + y + 1) * wide_m] = v.astype(BF16)

    def layer(m_ref, g, p):
        acc = None
        for c in range(3):
            part = jnp.dot(m_ref[c], g[c, 2 * p * wide_m : (2 * p + 4) * wide_m], preferred_element_type=F32)
            acc = part if acc is None else acc + part
        return acc

    for p in range(pairs2):
        acc = layer(m2_ref, g2, p)
        for y in range(2):
            value = jnp.maximum(acc[y * wide_m : (y + 1) * wide_m] + bias_of(1), 0.0)
            if p == 0 and y == 0:
                value = value * above
            if p == pairs2 - 1 and y == 1:
                value = value * below
            for c, v in enumerate(shifted(value)):
                g3[c, (2 * p + y) * wide_m : (2 * p + y + 1) * wide_m] = v.astype(BF16)

    for p in range(pairs3):
        acc = layer(m3_ref, g3, p)
        for y in range(2):
            staged[:, 2 * p + y, :] = jnp.maximum(acc[y * wide_m : (y + 1) * wide_m] + bias_of(2), 0.0)
    for z in range(Z):
        out_ref[:, z] = staged[z * C : (z + 1) * C].astype(BF16)


def on_device(tiles, entry_dest, entry_tile, entry_z, entry_xb, entry_ky, entry_kx, wy_table, wx_table,
              w_first, b_first, w_second, b_second, w_third, b_third):
    bricks = lax.axis_size("gy")
    entries = entry_dest.shape[0]
    per = entries // bricks
    n_tiles, sh, sw = tiles.shape
    dest = entry_dest.T
    tile, z, xb, ky, kx = (a.reshape(1, entries) for a in (entry_tile, entry_z, entry_xb, entry_ky, entry_kx))
    smem = pl.BlockSpec(memory_space=pltpu.SMEM)
    vmem = pl.BlockSpec(memory_space=pltpu.VMEM)
    kys = wy_table.shape[0]
    send = pl.pallas_call(
        functools.partial(send_kernel, per, "gy"),
        out_shape=jax.ShapeDtypeStruct((bricks * ROWS, sw), BF16),
        in_specs=[smem] * 4 + [vmem] * 3,
        out_specs=vmem,
        scratch_shapes=[pltpu.VMEM((kys, YB, n_tiles * sh), F32), pltpu.SMEM((bricks,), jnp.int32)],
        compiler_params=pltpu.CompilerParams(vmem_limit_bytes=24 * 1024 * 1024),
        name="send",
    )(dest, tile, ky, kx, tiles.reshape(n_tiles * sh, sw), wy_table.reshape(kys * YB, sh), wx_table.reshape(-1, sw))
    arrived = lax.all_to_all(send.reshape(bricks, ROWS, sw), "gy", split_axis=0, concat_axis=0, tiled=True)
    arrived = arrived.reshape(bricks * ROWS, sw)

    chunks = entries // LANES
    wide = LANES // per * ROWS
    rows = X // sw * ROWS
    w1 = w_first.transpose(1, 2, 3, 4, 0).reshape(9, 3, C)
    w2, w3 = (w.transpose(2, 3, 4, 0, 1).reshape(27, C, C) for w in (w_second, w_third))
    place, m1, m2, m3, bias = pl.pallas_call(
        functools.partial(prep_kernel, per, "gy"),
        out_shape=[
            jax.ShapeDtypeStruct((chunks, rows, wide), BF16),
            jax.ShapeDtypeStruct((2 * Z * C, 64), BF16),
            jax.ShapeDtypeStruct((3, 2 * Z * C, 4 * Z * C), BF16),
            jax.ShapeDtypeStruct((3, 2 * Z * C, 4 * Z * C), BF16),
            jax.ShapeDtypeStruct((3, Z * C, LANES), F32),
        ],
        in_specs=[vmem] * 9,
        out_specs=[vmem] * 5,
        scratch_shapes=[pltpu.VMEM((LANES, LANES), F32)],
        compiler_params=pltpu.CompilerParams(vmem_limit_bytes=24 * 1024 * 1024),
        cost_estimate=pl.CostEstimate(flops=200_000_000, bytes_accessed=3_000_000, transcendentals=0),
        name="prep",
    )(dest, z, xb, w1, b_first.reshape(1, C), w2, b_second.reshape(1, C), w3, b_third.reshape(1, C))

    return pl.pallas_call(
        functools.partial(conv_kernel, "gy", bricks),
        out_shape=jax.ShapeDtypeStruct((C, Z, YB, X), BF16),
        in_specs=[vmem] * 6,
        out_specs=vmem,
        scratch_shapes=[
            pltpu.VMEM((3, (YB + 4) * Z * C, X), BF16),
            pltpu.VMEM((3, (YB + 2) * Z * C, X), BF16),
            pltpu.VMEM((Z * C, YB, X), F32),
        ],
        compiler_params=pltpu.CompilerParams(vmem_limit_bytes=40 * 1024 * 1024),
        cost_estimate=pl.CostEstimate(flops=4_000_000_000, bytes_accessed=6_000_000, transcendentals=0),
        name="convs",
    )(arrived, place, m1, m2, m3, bias)


def solution(mesh):
    return jax.shard_map(
        on_device,
        mesh=mesh,
        in_specs=(
            P(("groups", "gy"), None, None),
            P("groups", None),
            P("groups"),
            P("groups"),
            P("groups"),
            P("groups"),
            P("groups"),
            P(),
            P(),
            P(),
            P(),
            P(),
            P(),
            P(),
            P(),
        ),
        out_specs=P(None, "groups", "gy", None),
        check_vma=False,
    )
```

```python
import functools

import jax
import jax.numpy as jnp
from jax import lax
from jax.experimental import pallas as pl
from jax.experimental.pallas import tpu as pltpu
from jax.sharding import PartitionSpec as P

X = 512
YB = 8
Z = 4
CAP = 4
C = 32
HALO = 3
YW = YB + 2 * HALO
CELLS = 16 * Z
LANES = 128
F32 = jnp.float32
BF16 = jnp.bfloat16


def payload_rows(per):
    rows = YW * CAP
    return rows if LANES // per * rows % 16 == 0 else -(-rows // 16) * 16


def iota(shape, dim):
    return lax.broadcasted_iota(jnp.int32, shape, dim)


def send_kernel(per, axis, dest_hbm, tile_hbm, ky_hbm, kx_hbm, tiles_hbm, wy_hbm, wx_hbm, out_ref,
                dest_ref, tile_ref, ky_ref, kx_ref, tiles_ref, wy_ref, wx_ref, wyt, count, sems):
    sources = (dest_hbm, tile_hbm, ky_hbm, kx_hbm, wy_hbm, tiles_hbm, wx_hbm)
    targets = (dest_ref, tile_ref, ky_ref, kx_ref, wy_ref, tiles_ref, wx_ref)
    copies = [pltpu.make_async_copy(a, b, sems.at[n]) for n, (a, b) in enumerate(zip(sources, targets))]
    for copy in copies:
        copy.start()
    bricks = count.shape[0]
    rows = out_ref.shape[0] // bricks
    base = lax.axis_index(axis) * per
    sh = wy_ref.shape[1]
    kys, kxs = wy_ref.shape[0] // YB, wx_ref.shape[0] // LANES
    cols = tiles_ref.shape[0]
    spread = (iota((sh, cols), 0) == iota((sh, cols), 1) % sh).astype(BF16)
    copies[4].wait()
    wyt[...] = jnp.dot(wy_ref[...], spread, preferred_element_type=F32).reshape(kys, YB, cols)

    def clear(i, carry):
        count[i] = 0
        return carry

    lax.fori_loop(0, bricks, clear, 0)
    for copy in copies[:4]:
        copy.wait()
    tile_of_col = iota((YB, cols), 1) // sh
    entry_of_lane = iota((YB, per * YB), 1) // YB
    key = jnp.zeros((YB, per * YB), jnp.int32)
    vertical, kinds = [], []
    for e in range(per):
        dest = dest_ref[0, base + e]
        rank = count[dest]
        count[dest] = rank + 1
        key = jnp.where(entry_of_lane == e, dest * (YB * CAP) + rank, key)
        vertical.append(jnp.where(tile_of_col == tile_ref[0, base + e], wyt[ky_ref[0, base + e]], 0.0))
        kinds.append(kx_ref[0, base + e])
    key = (key + CAP * (iota((YB, per * YB), 1) % YB))[:1]
    copies[5].wait()
    samples = jnp.dot(jnp.concatenate(vertical, axis=0).astype(BF16), tiles_ref[...], preferred_element_type=F32)
    samples = samples.astype(BF16).astype(F32)
    copies[6].wait()
    by_kind = []
    for k in range(kxs):
        by_kind.append(
            jnp.concatenate(
                [jnp.where(kinds[e] == k, samples[e * YB : (e + 1) * YB], 0.0) for e in range(per)], axis=0
            ).astype(BF16)
        )
    patches = jnp.dot(jnp.concatenate(by_kind, axis=1), wx_ref[...], preferred_element_type=F32).astype(BF16)
    block = LANES
    for j in range(bricks * rows // block):
        row = j * block + iota((block, per * YB), 0)
        row_key = (row // rows) * (YB * CAP) + row % rows - HALO * CAP
        chooser = (row_key == key).astype(F32).astype(BF16)
        out_ref[j * block : (j + 1) * block] = jnp.dot(chooser, patches, preferred_element_type=F32).astype(BF16)


def banded(w_ref, out_ref):
    wide = Z * C
    lane = iota((C, wide), 1)
    gap = jnp.zeros((C, wide - 3 * C), F32)
    for c in range(3):
        for b in range(3):
            taps = [w_ref[(a * 3 + b) * 3 + c].astype(F32) for a in range(3)]
            row = jnp.concatenate(taps + [gap], axis=1)
            rows = []
            for z in range(Z):
                moved = row if z == 1 else pltpu.roll(row, ((z - 1) * C) % wide, 1)
                if z == 0:
                    moved = jnp.where(lane < 2 * C, moved, 0.0)
                if z == Z - 1:
                    moved = jnp.where(lane >= (Z - 2) * C, moved, 0.0)
                rows.append(moved)
            at = (b * 3 + c) * wide
            out_ref[:, at : at + wide] = jnp.concatenate(rows, axis=0).astype(BF16)


def bias_rows(b_ref):
    column = jnp.sum(
        jnp.where(iota((C, C), 0) == iota((C, C), 1), jnp.broadcast_to(b_ref[...], (C, C)), 0.0), axis=1, keepdims=True
    )
    return jnp.concatenate([jnp.broadcast_to(column, (C, LANES))] * Z, axis=0)


def prep_kernel(per, axis, dest_ref, z_ref, xb_ref, w1_ref, b1_ref, w2_ref, b2_ref, w3_ref, b3_ref,
                place_ref, m1_ref, m2_ref, m3_ref, bias_ref, taps):
    own = lax.axis_index(axis)
    banded(w2_ref, m2_ref)
    banded(w3_ref, m3_ref)
    for n, b_ref in enumerate((b1_ref, b2_ref, b3_ref)):
        bias_ref[n] = bias_rows(b_ref)
    taps[...] = jnp.zeros_like(taps)
    for ab in range(9):
        taps[ab * 4 : ab * 4 + 3, :C] = w1_ref[ab].astype(F32)
    first = jnp.transpose(taps[...])[:C].astype(BF16)
    wide1 = m1_ref.shape[1]
    t = iota((LANES, wide1), 0)
    col = iota((LANES, wide1), 1)
    t_c, t_b, t_a = t % 4, (t // 4) % 3, t // 12
    for y in range(2):
        for z in range(Z):
            z_in = z + t_a - 1
            good = (t < 36) & (t_c < 3) & (z_in >= 0) & (z_in < Z)
            pick = (good & (col == t_c * (4 * Z) + (t_b + y) * Z + z_in)).astype(F32).astype(BF16)
            at = (y * Z + z) * C
            m1_ref[at : at + C, :] = jnp.dot(first, pick, preferred_element_type=F32).astype(BF16)
    chunks, rows, wide = place_ref.shape
    earlier = (
        (iota((LANES, LANES), 0) < iota((LANES, LANES), 1))
        & (iota((LANES, LANES), 0) // per == iota((LANES, LANES), 1) // per)
    ).astype(F32).astype(BF16)
    sent = payload_rows(per)
    slot_k, y_k, src_k = iota((wide, LANES), 0) % CAP, iota((wide, LANES), 0) % sent // CAP, iota((wide, LANES), 0) // sent
    same_source = src_k == iota((wide, LANES), 1) // per
    code_row = (iota((rows, LANES), 0) // CELLS) * Z + iota((rows, LANES), 0) % Z
    same_y = iota((rows, wide), 0) % CELLS // Z == iota((rows, wide), 1) % sent // CAP

    def one(n, carry):
        at = pl.multiple_of(n * LANES, LANES)
        dest = jnp.broadcast_to(dest_ref[:, pl.ds(at, LANES)], (8, LANES))
        code = xb_ref[:, pl.ds(at, LANES)] * Z + z_ref[:, pl.ds(at, LANES)]
        sub = iota((8, LANES), 0)
        named = (dest == own - 1 + sub) & (sub < 3)
        rank = jnp.dot(named.astype(F32).astype(BF16), earlier, preferred_element_type=F32).astype(jnp.int32)
        slot = jnp.where(named, rank, -1)
        wanted = jnp.where(y_k < HALO, slot[0:1], jnp.where(y_k < HALO + YB, slot[1:2], slot[2:3]))
        held = (same_source & (slot_k == wanted) & (y_k < YW)).astype(F32).astype(BF16)
        cell = (code_row == code).astype(F32).astype(BF16)
        hits = lax.dot_general(cell, held, (((1,), (1,)), ((), ())), preferred_element_type=F32)
        place_ref[n] = jnp.where(same_y, hits, 0.0).astype(BF16)
        return carry

    if chunks <= 8:
        for n in range(chunks):
            one(n, 0)
    else:
        lax.fori_loop(0, chunks, one, 0)


def shifted(values):
    lane = iota(values.shape, 1)
    last = values.shape[1] - 1
    zero = jnp.zeros_like(values)
    return (
        jnp.where(lane == 0, zero, pltpu.roll(values, 1, 1)),
        values,
        jnp.where(lane == last, zero, pltpu.roll(values, last, 1)),
    )


def conv_kernel(axis, bricks, arrived_ref, place_ref, m1_ref, m2_ref, m3_ref, bias_ref, out_ref,
                g2, g3, staged, packed, sems):
    own = lax.axis_index(axis)
    above, below = (own > 0).astype(F32), (own < bricks - 1).astype(F32)
    chunks, rows, wide = place_ref.shape
    wide_m = Z * C

    def place(n, total):
        at = n * wide if isinstance(n, int) else pl.multiple_of(n * wide, wide)
        return total + jnp.dot(place_ref[n], arrived_ref[pl.ds(at, wide)], preferred_element_type=F32)

    total = jnp.zeros((rows, LANES), F32)
    if chunks <= 8:
        for n in range(chunks):
            total = place(n, total)
    else:
        total = lax.fori_loop(0, chunks, place, total)
    image = jnp.concatenate([total[n * CELLS : (n + 1) * CELLS] for n in range(X // LANES)], axis=1)
    moved = shifted(image.astype(BF16).astype(F32))

    def bias_of(n, cols):
        return jnp.concatenate([bias_ref[n]] * (cols // LANES), axis=1)

    def keep(g, row, value):
        for c, v in enumerate(shifted(value.astype(BF16))):
            at = (row * 3 + c) * wide_m
            g[at : at + wide_m] = v

    def first(p):
        gathered = jnp.concatenate([m[2 * p * Z : (2 * p + 4) * Z] for m in moved], axis=0)
        gathered = jnp.concatenate([gathered, jnp.zeros((m1_ref.shape[1] - 12 * Z, X), F32)], axis=0).astype(BF16)
        acc = jnp.dot(m1_ref[...], gathered, preferred_element_type=F32)
        for y in range(2):
            value = jnp.maximum(acc[y * wide_m : (y + 1) * wide_m] + bias_of(0, X), 0.0)
            if p == 0:
                value = value * above
            if p == YB // 2 + 1:
                value = value * below
            keep(g2, 2 * p + y, value)

    def second(y):
        window = g2[3 * y * wide_m : 3 * (y + 3) * wide_m]
        value = jnp.maximum(jnp.dot(m2_ref[...], window, preferred_element_type=F32) + bias_of(1, X), 0.0)
        if y == 0:
            value = value * above
        if y == YB + 1:
            value = value * below
        keep(g3, y, value)

    parts, cols = packed.shape[0], packed.shape[4]

    def third(h, y):
        window = g3[3 * y * wide_m : 3 * (y + 3) * wide_m, h * cols : (h + 1) * cols]
        acc = jnp.dot(m3_ref[...], window, preferred_element_type=F32)
        staged[h, :, y, :] = jnp.maximum(acc + bias_of(2, cols), 0.0)

    def pack(h, z):
        packed[h, :, z] = staged[h, z * C : (z + 1) * C].astype(BF16)

    def send(h):
        return pltpu.make_async_copy(packed.at[h], out_ref.at[:, :, :, pl.ds(h * cols, cols)], sems.at[h])

    for p in range(YB // 2 + 2):
        first(p)
    for y in range(YB + 2):
        second(y)
    for h in range(parts):
        for y in range(YB):
            third(h, y)
        for z in range(Z):
            pack(h, z)
        send(h).start()
    for h in range(parts):
        send(h).wait()


def on_device(tiles, entry_dest, entry_tile, entry_z, entry_xb, entry_ky, entry_kx, wy_table, wx_table,
              w_first, b_first, w_second, b_second, w_third, b_third):
    bricks = lax.axis_size("gy")
    entries = entry_dest.shape[0]
    per = entries // bricks
    n_tiles, sh, sw = tiles.shape
    dest = entry_dest.T
    tile, z, xb, ky, kx = (a.reshape(1, entries) for a in (entry_tile, entry_z, entry_xb, entry_ky, entry_kx))
    hbm = pl.BlockSpec(memory_space=pl.ANY)
    vmem = pl.BlockSpec(memory_space=pltpu.VMEM)
    kys = wy_table.shape[0]
    sent = payload_rows(per)
    send = pl.pallas_call(
        functools.partial(send_kernel, per, "gy"),
        out_shape=jax.ShapeDtypeStruct((bricks * sent, sw), BF16),
        in_specs=[hbm] * 7,
        out_specs=vmem,
        scratch_shapes=[pltpu.SMEM((1, entries), jnp.int32)] * 4
        + [
            pltpu.VMEM((n_tiles * sh, sw), BF16),
            pltpu.VMEM((kys * YB, sh), BF16),
            pltpu.VMEM((wx_table.shape[0] * sw, sw), BF16),
            pltpu.VMEM((kys, YB, n_tiles * sh), F32),
            pltpu.SMEM((bricks,), jnp.int32),
            pltpu.SemaphoreType.DMA((7,)),
        ],
        compiler_params=pltpu.CompilerParams(vmem_limit_bytes=60 * 1024 * 1024),
        name="send",
    )(dest, tile, ky, kx, tiles.reshape(n_tiles * sh, sw), wy_table.reshape(kys * YB, sh), wx_table.reshape(-1, sw))
    arrived = lax.all_to_all(send.reshape(bricks, sent, sw), "gy", split_axis=0, concat_axis=0, tiled=True)
    arrived = arrived.reshape(bricks * sent, sw)

    chunks = entries // LANES
    wide = LANES // per * sent
    rows = X // sw * CELLS
    parts = 2
    w1 = w_first.transpose(1, 2, 3, 4, 0).reshape(9, 3, C)
    w2, w3 = (w.transpose(2, 3, 4, 0, 1).reshape(27, C, C) for w in (w_second, w_third))
    place, m1, m2, m3, bias = pl.pallas_call(
        functools.partial(prep_kernel, per, "gy"),
        out_shape=[
            jax.ShapeDtypeStruct((chunks, rows, wide), BF16),
            jax.ShapeDtypeStruct((2 * Z * C, 64), BF16),
            jax.ShapeDtypeStruct((Z * C, 9 * Z * C), BF16),
            jax.ShapeDtypeStruct((Z * C, 9 * Z * C), BF16),
            jax.ShapeDtypeStruct((3, Z * C, LANES), F32),
        ],
        in_specs=[vmem] * 9,
        out_specs=[vmem] * 5,
        scratch_shapes=[pltpu.VMEM((LANES, LANES), F32)],
        compiler_params=pltpu.CompilerParams(vmem_limit_bytes=24 * 1024 * 1024),
        cost_estimate=pl.CostEstimate(flops=200_000_000, bytes_accessed=3_000_000, transcendentals=0),
        name="prep",
    )(dest, z, xb, w1, b_first.reshape(1, C), w2, b_second.reshape(1, C), w3, b_third.reshape(1, C))

    return pl.pallas_call(
        functools.partial(conv_kernel, "gy", bricks),
        out_shape=jax.ShapeDtypeStruct((C, Z, YB, X), BF16),
        in_specs=[vmem] * 6,
        out_specs=pl.BlockSpec(memory_space=pl.ANY),
        scratch_shapes=[
            pltpu.VMEM((3 * (YB + 4) * Z * C, X), BF16),
            pltpu.VMEM((3 * (YB + 2) * Z * C, X), BF16),
            pltpu.VMEM((parts, Z * C, YB, X // parts), F32),
            pltpu.VMEM((parts, C, Z, YB, X // parts), BF16),
            pltpu.SemaphoreType.DMA((parts,)),
        ],
        compiler_params=pltpu.CompilerParams(vmem_limit_bytes=40 * 1024 * 1024),
        cost_estimate=pl.CostEstimate(flops=4_000_000_000, bytes_accessed=6_000_000, transcendentals=0),
        name="convs",
    )(arrived, place, m1, m2, m3, bias)


def solution(mesh):
    return jax.shard_map(
        on_device,
        mesh=mesh,
        in_specs=(
            P(("groups", "gy"), None, None),
            P("groups", None),
            P("groups"),
            P("groups"),
            P("groups"),
            P("groups"),
            P("groups"),
            P(),
            P(),
            P(),
            P(),
            P(),
            P(),
            P(),
            P(),
        ),
        out_specs=P(None, "groups", "gy", None),
        check_vma=False,
    )
```

```python
import functools

import jax
import jax.numpy as jnp
from jax import lax
from jax.experimental import pallas as pl
from jax.experimental.pallas import tpu as pltpu
from jax.sharding import PartitionSpec as P

X = 512
YB = 8
Z = 4
CAP = 4
C = 32
HALO = 3
YW = YB + 2 * HALO
CELLS = 16 * Z
LANES = 128
F32 = jnp.float32
BF16 = jnp.bfloat16


def payload_rows(per):
    rows = YW * CAP
    return rows if LANES // per * rows % 16 == 0 else -(-rows // 16) * 16


def iota(shape, dim):
    return lax.broadcasted_iota(jnp.int32, shape, dim)


def send_kernel(per, axis, dest_hbm, tile_hbm, ky_hbm, kx_hbm, tiles_hbm, wy_hbm, wx_hbm, out_ref,
                dest_ref, tile_ref, ky_ref, kx_ref, tiles_ref, wy_ref, wx_ref, wyt, sorted_by, placed, count, sems):
    sources = (dest_hbm, tile_hbm, ky_hbm, kx_hbm, wy_hbm, tiles_hbm, wx_hbm)
    targets = (dest_ref, tile_ref, ky_ref, kx_ref, wy_ref, tiles_ref, wx_ref)
    copies = [pltpu.make_async_copy(a, b, sems.at[n]) for n, (a, b) in enumerate(zip(sources, targets))]
    for copy in copies:
        copy.start()

    bricks = count.shape[0]
    rows = out_ref.shape[0] // bricks
    base = lax.axis_index(axis) * per
    sh = wy_ref.shape[1]
    kys, fold = wy_ref.shape[0] // YB, sorted_by.shape[0]

    def blank(k, carry):
        sorted_by[k] = jnp.zeros(sorted_by.shape[1:], F32)
        return carry

    def clear(i, carry):
        count[i] = 0
        return carry

    def blank_placed(k, carry):
        placed[pl.ds(pl.multiple_of(k * rows, 8), rows)] = jnp.zeros((rows, placed.shape[1]), F32)
        return carry

    lax.fori_loop(0, sorted_by.shape[0], blank, 0)
    lax.fori_loop(0, bricks + 2, blank_placed, 0)
    lax.fori_loop(0, count.shape[0], clear, 0)
    group = min(per, 16)
    copies[4].wait()
    spread = (iota((sh, group * sh), 0) == iota((sh, group * sh), 1) % sh).astype(F32).astype(BF16)
    wyt[...] = jnp.dot(wy_ref[...], spread, preferred_element_type=F32).reshape(kys, YB, group * sh)
    for copy in copies[:4]:
        copy.wait()
    entry_of_col = iota((YB, group * sh), 1) // sh
    vertical = [jnp.where(entry_of_col == e % group, wyt[ky_ref[0, base + e]], 0.0) for e in range(per)]
    copies[5].wait()
    for g in range(0, per, group):
        picked = [tiles_ref[pl.ds(pl.multiple_of(tile_ref[0, base + e] * sh, sh), sh)] for e in range(g, g + group)]
        weights = jnp.concatenate(vertical[g : g + group], axis=0).astype(BF16)
        samples = jnp.dot(weights, jnp.concatenate(picked, axis=0), preferred_element_type=F32)
        samples = samples.astype(BF16).astype(F32)
        for e in range(g, g + group):
            sorted_by[kx_ref[0, base + e] % fold, e * YB : (e + 1) * YB] = samples[(e - g) * YB : (e - g + 1) * YB]
    copies[6].wait()
    by_kind = jnp.concatenate([sorted_by[k].astype(BF16) for k in range(fold)], axis=1)
    sides = [wx_ref[: fold * LANES], wx_ref[fold * LANES :]]
    patches = jnp.dot(by_kind, jnp.concatenate(sides, axis=1), preferred_element_type=F32)
    for e in range(per):
        dest = dest_ref[0, base + e]
        rank = count[dest]
        count[dest] = rank + 1
        at = (dest + 1) * rows + rank
        patch = patches[e * YB : (e + 1) * YB]
        patch = jnp.where(kx_ref[0, base + e] < fold, patch[:, :LANES], patch[:, LANES:])
        placed[pl.ds(at + HALO * CAP, YB, stride=CAP)] = patch
        placed[pl.ds(at + rows, HALO, stride=CAP)] = patch[YB - HALO :]
        placed[pl.ds(at - rows + (HALO + YB) * CAP, HALO, stride=CAP)] = patch[:HALO]
    out_ref[...] = placed[rows : rows + out_ref.shape[0]].astype(BF16)


def banded(w_ref, out_ref, rest_ref):
    hole = jnp.zeros((C, C), F32)

    def tap(a, b, c):
        return w_ref[(a * 3 + b) * 3 + c].astype(F32)

    for b in range(3):
        taps = [[tap(a, b, c) for a in range(3)] for c in range(3)]
        far = [piece for p in taps for piece in (p[1], p[2])]
        near = [piece for p in taps for piece in (p[0], p[1])]
        uppers = (far + [hole, hole], near + [taps[0][2], taps[1][2]])
        lowers = (far + [taps[0][0], taps[1][0]], near + [hole, hole])
        for n, rows in enumerate((uppers, lowers)):
            block = jnp.concatenate([jnp.concatenate(row, axis=1) for row in rows], axis=0)
            out_ref[n, b * 2 * C : (b + 1) * 2 * C] = block.astype(BF16)
    for y in range(6):
        reach = [r - y + 2 for r in range(4)]
        one = [piece for b in reach for piece in (tap(2, b, 2) if 0 <= b <= 2 else hole, hole)]
        two = [piece for b in reach for piece in (hole, tap(0, b, 2) if 0 <= b <= 2 else hole)]
        block = jnp.concatenate([jnp.concatenate(one, axis=1), jnp.concatenate(two, axis=1)], axis=0)
        rest_ref[y * 2 * C : (y + 1) * 2 * C] = block.astype(BF16)


def bias_rows(b_ref):
    column = jnp.sum(
        jnp.where(iota((C, C), 0) == iota((C, C), 1), jnp.broadcast_to(b_ref[...], (C, C)), 0.0), axis=1, keepdims=True
    )
    return jnp.concatenate([jnp.broadcast_to(column, (C, LANES))] * Z, axis=0)


def prep_kernel(per, axis, dest_ref, z_ref, xb_ref, w1_ref, b1_ref, w2_ref, b2_ref, w3_ref, b3_ref,
                place_ref, m1_ref, m2_ref, r2_ref, m3_ref, r3_ref, bias_ref, taps):
    own = lax.axis_index(axis)
    banded(w2_ref, m2_ref, r2_ref)
    banded(w3_ref, m3_ref, r3_ref)
    for n, b_ref in enumerate((b1_ref, b2_ref, b3_ref)):
        bias_ref[n] = bias_rows(b_ref)
    taps[...] = jnp.zeros_like(taps)
    for ab in range(9):
        taps[ab * 4 : ab * 4 + 3, :C] = w1_ref[ab].astype(F32)
    first = jnp.transpose(taps[...])[:C].astype(BF16)
    wide1 = m1_ref.shape[1]
    t = iota((LANES, wide1), 0)
    col = iota((LANES, wide1), 1)
    t_c, t_b, t_a = t % 4, (t // 4) % 3, t // 12
    for y in range(2):
        for z in range(Z):
            z_in = z + t_a - 1
            good = (t < 36) & (t_c < 3) & (z_in >= 0) & (z_in < Z)
            pick = (good & (col == t_c * (4 * Z) + (t_b + y) * Z + z_in)).astype(F32).astype(BF16)
            at = (y * Z + z) * C
            m1_ref[at : at + C, :] = jnp.dot(first, pick, preferred_element_type=F32).astype(BF16)
    chunks, rows, wide = place_ref.shape
    earlier = (
        (iota((LANES, LANES), 0) < iota((LANES, LANES), 1))
        & (iota((LANES, LANES), 0) // per == iota((LANES, LANES), 1) // per)
    ).astype(F32).astype(BF16)
    sent = payload_rows(per)
    slot_k, y_k, src_k = iota((wide, LANES), 0) % CAP, iota((wide, LANES), 0) % sent // CAP, iota((wide, LANES), 0) // sent
    same_source = src_k == iota((wide, LANES), 1) // per
    code_row = (iota((rows, LANES), 0) // CELLS) * Z + iota((rows, LANES), 0) % Z
    same_y = iota((rows, wide), 0) % CELLS // Z == iota((rows, wide), 1) % sent // CAP

    def one(n, carry):
        at = pl.multiple_of(n * LANES, LANES)
        dest = jnp.broadcast_to(dest_ref[:, pl.ds(at, LANES)], (8, LANES))
        code = xb_ref[:, pl.ds(at, LANES)] * Z + z_ref[:, pl.ds(at, LANES)]
        sub = iota((8, LANES), 0)
        named = (dest == own - 1 + sub) & (sub < 3)
        rank = jnp.dot(named.astype(F32).astype(BF16), earlier, preferred_element_type=F32).astype(jnp.int32)
        slot = jnp.where(named, rank, -1)
        wanted = jnp.where(y_k < HALO, slot[0:1], jnp.where(y_k < HALO + YB, slot[1:2], slot[2:3]))
        held = (same_source & (slot_k == wanted) & (y_k < YW)).astype(F32).astype(BF16)
        cell = (code_row == code).astype(F32).astype(BF16)
        hits = lax.dot_general(cell, held, (((1,), (1,)), ((), ())), preferred_element_type=F32)
        place_ref[n] = jnp.where(same_y, hits, 0.0).astype(BF16)
        return carry

    if chunks <= 8:
        for n in range(chunks):
            one(n, 0)
    else:
        lax.fori_loop(0, chunks, one, 0)


def shifted(values):
    lane = iota(values.shape, 1)
    last = values.shape[1] - 1
    zero = jnp.zeros_like(values)
    return (
        jnp.where(lane == 0, zero, pltpu.roll(values, 1, 1)),
        values,
        jnp.where(lane == last, zero, pltpu.roll(values, last, 1)),
    )


def conv_kernel(axis, bricks, arrived_ref, place_ref, m1_ref, m2_ref, r2_ref, m3_ref, r3_ref, bias_ref, out_ref,
                g2, e2, g3, e3, staged, packed, sems):
    own = lax.axis_index(axis)
    above, below = (own > 0).astype(F32), (own < bricks - 1).astype(F32)
    chunks, rows, wide = place_ref.shape
    wide_m, half = Z * C, Z * C // 2

    def place(n, total):
        at = n * wide if isinstance(n, int) else pl.multiple_of(n * wide, wide)
        return total + jnp.dot(place_ref[n], arrived_ref[pl.ds(at, wide)], preferred_element_type=F32)

    total = jnp.zeros((rows, LANES), F32)
    if chunks <= 8:
        for n in range(chunks):
            total = place(n, total)
    else:
        total = lax.fori_loop(0, chunks, place, total)
    image = jnp.concatenate([total[n * CELLS : (n + 1) * CELLS] for n in range(X // LANES)], axis=1)
    moved = shifted(image.astype(BF16).astype(F32))

    def bias_of(n, cols):
        return jnp.concatenate([bias_ref[n]] * (cols // LANES), axis=1)

    def keep(g, e, row, value):
        at = 8 * C * row
        for c, v in enumerate(shifted(value.astype(BF16))):
            g[0, at + c * half : at + (c + 1) * half] = v[:half]
            g[1, at + c * half : at + (c + 1) * half] = v[half:]
            if c < 2:
                g[0, at + (6 + c) * C : at + (7 + c) * C] = v[2 * C : 3 * C]
                g[1, at + (6 + c) * C : at + (7 + c) * C] = v[C : 2 * C]
            else:
                e[row * half : row * half + C] = v[2 * C : 3 * C]
                e[row * half + C : (row + 1) * half] = v[C : 2 * C]

    def first(p):
        gathered = jnp.concatenate([m[2 * p * Z : (2 * p + 4) * Z] for m in moved], axis=0)
        gathered = jnp.concatenate([gathered, jnp.zeros((m1_ref.shape[1] - 12 * Z, X), F32)], axis=0).astype(BF16)
        acc = jnp.dot(m1_ref[...], gathered, preferred_element_type=F32)
        for y in range(2):
            value = jnp.maximum(acc[y * wide_m : (y + 1) * wide_m] + bias_of(0, X), 0.0)
            if p == 0:
                value = value * above
            if p == YB // 2 + 1:
                value = value * below
            keep(g2, e2, 2 * p + y, value)

    def layer(m_ref, r_ref, g, e, rows_in, at, cols, finish):
        sums = {y: [] for y in range(rows_in - 2)}
        there = slice(at, at + cols)

        def rest(r):
            count = min(4, rows_in - r)
            low, high = max(0, r - 2), min(rows_in - 2, r + count)
            taps = slice((low - r + 2) * half, (high - r + 2) * half)
            found = jnp.dot(r_ref[taps, : count * half], e[r * half : (r + count) * half, there], preferred_element_type=F32)
            for y in range(low, high):
                sums[y].append((C, found[(y - low) * half : (y - low + 1) * half]))

        for r in range(rows_in):
            if r % 4 == 0:
                rest(r)
            low, high = max(0, r - rows_in + 3), min(2, r)
            taps = slice(low * half, (high + 1) * half)
            window = slice(8 * C * r, 8 * C * (r + 1))
            for n in range(2):
                found = jnp.dot(m_ref[n, taps], g[n, window, there], preferred_element_type=F32)
                for b in range(low, high + 1):
                    sums[r - b].append((n * half, found[(b - low) * half : (b - low + 1) * half]))
            if r >= 2:
                pieces = []
                for z in range(Z):
                    parts_z = [v[z * C - o : z * C - o + C] for o, v in sums[r - 2] if o <= z * C < o + half]
                    pieces.append(functools.reduce(lambda p, q: p + q, parts_z))
                finish(r - 2, jnp.concatenate(pieces, axis=0))

    def second(y, total):
        value = jnp.maximum(total + bias_of(1, X), 0.0)
        if y == 0:
            value = value * above
        if y == YB + 1:
            value = value * below
        keep(g3, e3, y, value)

    parts, cols = packed.shape[0], packed.shape[4]

    def third(h, y, total):
        value = jnp.maximum(total + bias_of(2, cols), 0.0)
        for k in range(cols // LANES):
            staged[h, k, pl.ds(y, wide_m, stride=YB), :] = value[:, k * LANES : (k + 1) * LANES]
        if h > 0 and y == YB // 2 - 1:
            flush(h - 1)

    def pack(h, z):
        for k in range(cols // LANES):
            turned = staged[h, k, z * C * YB : (z + 1) * C * YB].astype(BF16).reshape(C, YB, LANES)
            packed[h, z, :, :, k * LANES : (k + 1) * LANES] = turned

    def send(h, z):
        there = out_ref.at[:, z, :, pl.ds(h * cols, cols)]
        return pltpu.make_async_copy(packed.at[h, z], there, sems.at[h, z])

    for p in range(YB // 2 + 2):
        first(p)
    def flush(h):
        for z in range(Z):
            pack(h, z)
            send(h, z).start()

    layer(m2_ref, r2_ref, g2, e2, YB + 4, 0, X, second)
    for h in range(parts):
        layer(m3_ref, r3_ref, g3, e3, YB + 2, h * cols, cols, functools.partial(third, h))

    @pl.when(own >= 0)
    def _():
        flush(parts - 1)

    for h in range(parts):
        for z in range(Z):
            send(h, z).wait()


def on_device(tiles, entry_dest, entry_tile, entry_z, entry_xb, entry_ky, entry_kx, wy_table, wx_table,
              w_first, b_first, w_second, b_second, w_third, b_third):
    bricks = lax.axis_size("gy")
    entries = entry_dest.shape[0]
    per = entries // bricks
    n_tiles, sh, sw = tiles.shape
    dest = entry_dest.T
    tile, z, xb, ky, kx = (a.reshape(1, entries) for a in (entry_tile, entry_z, entry_xb, entry_ky, entry_kx))
    hbm = pl.BlockSpec(memory_space=pl.ANY)
    vmem = pl.BlockSpec(memory_space=pltpu.VMEM)
    kys = wy_table.shape[0]
    sent = payload_rows(per)
    send = pl.pallas_call(
        functools.partial(send_kernel, per, "gy"),
        out_shape=jax.ShapeDtypeStruct((bricks * sent, sw), BF16),
        in_specs=[hbm] * 7,
        out_specs=vmem,
        scratch_shapes=[pltpu.SMEM((1, entries), jnp.int32)] * 4
        + [
            pltpu.VMEM((n_tiles * sh, sw), BF16),
            pltpu.VMEM((kys * YB, sh), BF16),
            pltpu.VMEM((wx_table.shape[0] * sw, sw), BF16),
            pltpu.VMEM((kys, YB, min(per, 16) * sh), F32),
            pltpu.VMEM((wx_table.shape[0] // 2, per * YB, sw), F32),
            pltpu.VMEM(((bricks + 2) * sent, sw), F32),
            pltpu.SMEM((bricks,), jnp.int32),
            pltpu.SemaphoreType.DMA((7,)),
        ],
        compiler_params=pltpu.CompilerParams(vmem_limit_bytes=60 * 1024 * 1024),
        name="send",
    )(dest, tile, ky, kx, tiles.reshape(n_tiles * sh, sw), wy_table.reshape(kys * YB, sh), wx_table.reshape(-1, sw))
    arrived = lax.all_to_all(send.reshape(bricks, sent, sw), "gy", split_axis=0, concat_axis=0, tiled=True)
    arrived = arrived.reshape(bricks * sent, sw)

    chunks = entries // LANES
    wide = LANES // per * sent
    rows = X // sw * CELLS
    parts = 2
    w1 = w_first.transpose(1, 2, 3, 4, 0).reshape(9, 3, C)
    w2, w3 = (w.transpose(2, 3, 4, 0, 1).reshape(27, C, C) for w in (w_second, w_third))
    place, m1, m2, r2, m3, r3, bias = pl.pallas_call(
        functools.partial(prep_kernel, per, "gy"),
        out_shape=[
            jax.ShapeDtypeStruct((chunks, rows, wide), BF16),
            jax.ShapeDtypeStruct((2 * Z * C, 64), BF16),
            jax.ShapeDtypeStruct((2, 6 * C, 8 * C), BF16),
            jax.ShapeDtypeStruct((12 * C, 8 * C), BF16),
            jax.ShapeDtypeStruct((2, 6 * C, 8 * C), BF16),
            jax.ShapeDtypeStruct((12 * C, 8 * C), BF16),
            jax.ShapeDtypeStruct((3, Z * C, LANES), F32),
        ],
        in_specs=[vmem] * 9,
        out_specs=[vmem] * 7,
        scratch_shapes=[pltpu.VMEM((LANES, LANES), F32)],
        compiler_params=pltpu.CompilerParams(vmem_limit_bytes=24 * 1024 * 1024),
        cost_estimate=pl.CostEstimate(flops=200_000_000, bytes_accessed=3_000_000, transcendentals=0),
        name="prep",
    )(dest, z, xb, w1, b_first.reshape(1, C), w2, b_second.reshape(1, C), w3, b_third.reshape(1, C))

    return pl.pallas_call(
        functools.partial(conv_kernel, "gy", bricks),
        out_shape=jax.ShapeDtypeStruct((C, Z, YB, X), BF16),
        in_specs=[vmem] * 8,
        out_specs=pl.BlockSpec(memory_space=pl.ANY),
        scratch_shapes=[
            pltpu.VMEM((2, (YB + 4) * 8 * C, X), BF16),
            pltpu.VMEM(((YB + 4) * 2 * C, X), BF16),
            pltpu.VMEM((2, (YB + 2) * 8 * C, X), BF16),
            pltpu.VMEM(((YB + 2) * 2 * C, X), BF16),
            pltpu.VMEM((parts, X // parts // LANES, Z * C * YB, LANES), F32),
            pltpu.VMEM((parts, Z, C, YB, X // parts), BF16),
            pltpu.SemaphoreType.DMA((parts, Z)),
        ],
        compiler_params=pltpu.CompilerParams(vmem_limit_bytes=40 * 1024 * 1024),
        cost_estimate=pl.CostEstimate(flops=4_000_000_000, bytes_accessed=6_000_000, transcendentals=0),
        name="convs",
    )(arrived, place, m1, m2, r2, m3, r3, bias)


def solution(mesh):
    return jax.shard_map(
        on_device,
        mesh=mesh,
        in_specs=(
            P(("groups", "gy"), None, None),
            P("groups", None),
            P("groups"),
            P("groups"),
            P("groups"),
            P("groups"),
            P("groups"),
            P(),
            P(),
            P(),
            P(),
            P(),
            P(),
            P(),
            P(),
        ),
        out_specs=P(None, "groups", "gy", None),
        check_vma=False,
    )
```

```python
import functools

import jax
import jax.numpy as jnp
from jax import lax
from jax.experimental import pallas as pl
from jax.experimental.pallas import tpu as pltpu
from jax.sharding import PartitionSpec as P

X = 512
YB = 8
Z = 4
CAP = 4
C = 32
HALO = 3
YW = YB + 2 * HALO
CELLS = YW * Z
LANES = 128
F32 = jnp.float32
BF16 = jnp.bfloat16


def payload_rows(per):
    rows = YW * CAP
    return rows if LANES // per * rows % 16 == 0 else -(-rows // 16) * 16


def iota(shape, dim):
    return lax.broadcasted_iota(jnp.int32, shape, dim)


def send_kernel(per, axis, dest_hbm, tile_hbm, ky_hbm, kx_hbm, tiles_hbm, wy_hbm, wx_hbm, out_ref,
                dest_ref, tile_ref, ky_ref, kx_ref, tiles_ref, wy_ref, wx_ref, wyt, sorted_by, placed, count, sems):
    sources = (dest_hbm, tile_hbm, ky_hbm, kx_hbm, wy_hbm, tiles_hbm, wx_hbm)
    targets = (dest_ref, tile_ref, ky_ref, kx_ref, wy_ref, tiles_ref, wx_ref)
    copies = [pltpu.make_async_copy(a, b, sems.at[n]) for n, (a, b) in enumerate(zip(sources, targets))]
    for copy in copies:
        copy.start()

    bricks = count.shape[0]
    rows = out_ref.shape[0] // bricks
    base = lax.axis_index(axis) * per
    sh = wy_ref.shape[1]
    kys, fold = wy_ref.shape[0] // YB, sorted_by.shape[0]

    def blank(k, carry):
        sorted_by[k] = jnp.zeros(sorted_by.shape[1:], F32)
        return carry

    def clear(i, carry):
        count[i] = 0
        return carry

    def blank_placed(k, carry):
        placed[pl.ds(pl.multiple_of(k * rows, 8), rows)] = jnp.zeros((rows, placed.shape[1]), F32)
        return carry

    lax.fori_loop(0, sorted_by.shape[0], blank, 0)
    lax.fori_loop(0, bricks + 2, blank_placed, 0)
    lax.fori_loop(0, count.shape[0], clear, 0)
    group = min(per, 16)
    copies[4].wait()
    spread = (iota((sh, group * sh), 0) == iota((sh, group * sh), 1) % sh).astype(F32).astype(BF16)
    wyt[...] = jnp.dot(wy_ref[...], spread, preferred_element_type=F32).reshape(kys, YB, group * sh)
    for copy in copies[:4]:
        copy.wait()
    entry_of_col = iota((YB, group * sh), 1) // sh
    vertical = [jnp.where(entry_of_col == e % group, wyt[ky_ref[0, base + e]], 0.0) for e in range(per)]
    copies[5].wait()
    for g in range(0, per, group):
        picked = [tiles_ref[pl.ds(pl.multiple_of(tile_ref[0, base + e] * sh, sh), sh)] for e in range(g, g + group)]
        weights = jnp.concatenate(vertical[g : g + group], axis=0).astype(BF16)
        samples = jnp.dot(weights, jnp.concatenate(picked, axis=0), preferred_element_type=F32)
        samples = samples.astype(BF16).astype(F32)
        for e in range(g, g + group):
            sorted_by[kx_ref[0, base + e] % fold, e * YB : (e + 1) * YB] = samples[(e - g) * YB : (e - g + 1) * YB]
    copies[6].wait()
    by_kind = jnp.concatenate([sorted_by[k].astype(BF16) for k in range(fold)], axis=1)
    sides = [wx_ref[: fold * LANES], wx_ref[fold * LANES :]]
    patches = jnp.dot(by_kind, jnp.concatenate(sides, axis=1), preferred_element_type=F32)
    for e in range(per):
        dest = dest_ref[0, base + e]
        rank = count[dest]
        count[dest] = rank + 1
        at = (dest + 1) * rows + rank
        patch = patches[e * YB : (e + 1) * YB]
        patch = jnp.where(kx_ref[0, base + e] < fold, patch[:, :LANES], patch[:, LANES:])
        placed[pl.ds(at + HALO * CAP, YB, stride=CAP)] = patch
        placed[pl.ds(at + rows, HALO, stride=CAP)] = patch[YB - HALO :]
        placed[pl.ds(at - rows + (HALO + YB) * CAP, HALO, stride=CAP)] = patch[:HALO]
    out_ref[...] = placed[rows : rows + out_ref.shape[0]].astype(BF16)


def banded(w_ref, out_ref, rest_ref):
    hole = jnp.zeros((C, C), F32)

    def tap(a, b, c):
        return w_ref[(a * 3 + b) * 3 + c].astype(F32)

    for b in range(3):
        taps = [[tap(a, b, c) for a in range(3)] for c in range(3)]
        far = [piece for p in taps for piece in (p[1], p[2])]
        near = [piece for p in taps for piece in (p[0], p[1])]
        uppers = (far + [hole, hole], near + [taps[0][2], taps[1][2]])
        lowers = (far + [taps[0][0], taps[1][0]], near + [hole, hole])
        for n, rows in enumerate((uppers, lowers)):
            block = jnp.concatenate([jnp.concatenate(row, axis=1) for row in rows], axis=0)
            out_ref[n, b * 2 * C : (b + 1) * 2 * C] = block.astype(BF16)
    for y in range(6):
        reach = [r - y + 2 for r in range(4)]
        one = [piece for b in reach for piece in (tap(2, b, 2) if 0 <= b <= 2 else hole, hole)]
        two = [piece for b in reach for piece in (hole, tap(0, b, 2) if 0 <= b <= 2 else hole)]
        block = jnp.concatenate([jnp.concatenate(one, axis=1), jnp.concatenate(two, axis=1)], axis=0)
        rest_ref[y * 2 * C : (y + 1) * 2 * C] = block.astype(BF16)


def bias_rows(b_ref):
    column = jnp.sum(
        jnp.where(iota((C, C), 0) == iota((C, C), 1), jnp.broadcast_to(b_ref[...], (C, C)), 0.0), axis=1, keepdims=True
    )
    return jnp.concatenate([jnp.broadcast_to(column, (C, LANES))] * Z, axis=0)


def prep_kernel(per, axis, dest_ref, z_ref, xb_ref, w1_ref, b1_ref, w2_ref, b2_ref, w3_ref, b3_ref,
                place_ref, m1_ref, m2_ref, r2_ref, m3_ref, r3_ref, bias_ref, taps):
    own = lax.axis_index(axis)
    banded(w2_ref, m2_ref, r2_ref)
    banded(w3_ref, m3_ref, r3_ref)
    for n, b_ref in enumerate((b1_ref, b2_ref, b3_ref)):
        bias_ref[n] = bias_rows(b_ref)
    taps[...] = jnp.zeros_like(taps)
    for ab in range(9):
        taps[ab * 4 : ab * 4 + 3, :C] = w1_ref[ab].astype(F32)
    first = jnp.transpose(taps[...])[:C].astype(BF16)
    wide1 = m1_ref.shape[1]
    t = iota((LANES, wide1), 0)
    col = iota((LANES, wide1), 1)
    t_c, t_b, t_a = t % 4, (t // 4) % 3, t // 12
    for y in range(2):
        for z in range(Z):
            z_in = z + t_a - 1
            good = (t < 36) & (t_c < 3) & (z_in >= 0) & (z_in < Z)
            pick = (good & (col == t_c * (4 * Z) + (t_b + y) * Z + z_in)).astype(F32).astype(BF16)
            at = (y * Z + z) * C
            m1_ref[at : at + C, :] = jnp.dot(first, pick, preferred_element_type=F32).astype(BF16)
    chunks, rows, wide = place_ref.shape
    earlier = (
        (iota((LANES, LANES), 0) < iota((LANES, LANES), 1))
        & (iota((LANES, LANES), 0) // per == iota((LANES, LANES), 1) // per)
    ).astype(F32).astype(BF16)
    sent = payload_rows(per)
    slot_k, y_k, src_k = iota((wide, LANES), 0) % CAP, iota((wide, LANES), 0) % sent // CAP, iota((wide, LANES), 0) // sent
    same_source = src_k == iota((wide, LANES), 1) // per
    code_row = (iota((rows, LANES), 0) // CELLS) * Z + iota((rows, LANES), 0) % Z
    same_y = iota((rows, wide), 0) % CELLS // Z == iota((rows, wide), 1) % sent // CAP

    def one(n, carry):
        at = pl.multiple_of(n * LANES, LANES)
        dest = jnp.broadcast_to(dest_ref[:, pl.ds(at, LANES)], (8, LANES))
        code = xb_ref[:, pl.ds(at, LANES)] * Z + z_ref[:, pl.ds(at, LANES)]
        sub = iota((8, LANES), 0)
        named = (dest == own - 1 + sub) & (sub < 3)
        rank = jnp.dot(named.astype(F32).astype(BF16), earlier, preferred_element_type=F32).astype(jnp.int32)
        slot = jnp.where(named, rank, -1)
        wanted = jnp.where(y_k < HALO, slot[0:1], jnp.where(y_k < HALO + YB, slot[1:2], slot[2:3]))
        held = (same_source & (slot_k == wanted) & (y_k < YW)).astype(F32).astype(BF16)
        cell = (code_row == code).astype(F32).astype(BF16)
        hits = lax.dot_general(cell, held, (((1,), (1,)), ((), ())), preferred_element_type=F32)
        place_ref[n] = jnp.where(same_y, hits, 0.0).astype(BF16)
        return carry

    if chunks <= 8:
        for n in range(chunks):
            one(n, 0)
    else:
        lax.fori_loop(0, chunks, one, 0)


def shifted(values):
    lane = iota(values.shape, 1)
    last = values.shape[1] - 1
    zero = jnp.zeros_like(values)
    return (
        jnp.where(lane == 0, zero, pltpu.roll(values, 1, 1)),
        values,
        jnp.where(lane == last, zero, pltpu.roll(values, last, 1)),
    )


def conv_kernel(axis, bricks, arrived_ref, place_ref, m1_ref, m2_ref, r2_ref, m3_ref, r3_ref, bias_ref, out_ref,
                g2, e2, g3, e3, staged, packed, sems):
    own = lax.axis_index(axis)
    above, below = (own > 0).astype(F32), (own < bricks - 1).astype(F32)
    chunks, rows, wide = place_ref.shape
    wide_m, half = Z * C, Z * C // 2

    def place(n, total):
        at = n * wide if isinstance(n, int) else pl.multiple_of(n * wide, wide)
        return total + jnp.dot(place_ref[n], arrived_ref[pl.ds(at, wide)], preferred_element_type=F32)

    total = jnp.zeros((rows, LANES), F32)
    if chunks <= 8:
        for n in range(chunks):
            total = place(n, total)
    else:
        total = lax.fori_loop(0, chunks, place, total)
    image = jnp.concatenate([total[n * CELLS : (n + 1) * CELLS] for n in range(X // LANES)], axis=1)
    moved = shifted(image.astype(BF16).astype(F32))

    def bias_of(n, cols):
        return jnp.concatenate([bias_ref[n]] * (cols // LANES), axis=1)

    def keep(g, e, row, value):
        at = 8 * C * row
        for c, v in enumerate(shifted(value.astype(BF16))):
            g[0, at + c * half : at + (c + 1) * half] = v[:half]
            g[1, at + c * half : at + (c + 1) * half] = v[half:]
            if c < 2:
                g[0, at + (6 + c) * C : at + (7 + c) * C] = v[2 * C : 3 * C]
                g[1, at + (6 + c) * C : at + (7 + c) * C] = v[C : 2 * C]
            else:
                e[row * half : row * half + C] = v[2 * C : 3 * C]
                e[row * half + C : (row + 1) * half] = v[C : 2 * C]

    def first(p):
        gathered = jnp.concatenate([m[2 * p * Z : (2 * p + 4) * Z] for m in moved], axis=0)
        gathered = jnp.concatenate([gathered, jnp.zeros((m1_ref.shape[1] - 12 * Z, X), F32)], axis=0).astype(BF16)
        acc = jnp.dot(m1_ref[...], gathered, preferred_element_type=F32)
        for y in range(2):
            value = jnp.maximum(acc[y * wide_m : (y + 1) * wide_m] + bias_of(0, X), 0.0)
            if p == 0:
                value = value * above
            if p == YB // 2 + 1:
                value = value * below
            keep(g2, e2, 2 * p + y, value)

    def layer(m_ref, r_ref, g, e, rows_in, at, cols, finish):
        sums = {y: [] for y in range(rows_in - 2)}
        there = slice(at, at + cols)

        def rest(r):
            count = min(4, rows_in - r)
            low, high = max(0, r - 2), min(rows_in - 2, r + count)
            taps = slice((low - r + 2) * half, (high - r + 2) * half)
            found = jnp.dot(r_ref[taps, : count * half], e[r * half : (r + count) * half, there], preferred_element_type=F32)
            for y in range(low, high):
                sums[y].append((C, found[(y - low) * half : (y - low + 1) * half]))

        for r in range(rows_in):
            if r % 4 == 0:
                rest(r)
            low, high = max(0, r - rows_in + 3), min(2, r)
            taps = slice(low * half, (high + 1) * half)
            window = slice(8 * C * r, 8 * C * (r + 1))
            for n in range(2):
                found = jnp.dot(m_ref[n, taps], g[n, window, there], preferred_element_type=F32)
                for b in range(low, high + 1):
                    sums[r - b].append((n * half, found[(b - low) * half : (b - low + 1) * half]))
            if r >= 2:
                pieces = []
                for z in range(Z):
                    parts_z = [v[z * C - o : z * C - o + C] for o, v in sums[r - 2] if o <= z * C < o + half]
                    pieces.append(functools.reduce(lambda p, q: p + q, parts_z))
                finish(r - 2, jnp.concatenate(pieces, axis=0))

    def second(y, total):
        value = jnp.maximum(total + bias_of(1, X), 0.0)
        if y == 0:
            value = value * above
        if y == YB + 1:
            value = value * below
        keep(g3, e3, y, value)

    parts, cols = packed.shape[0], packed.shape[4]

    def third(h, y, total):
        value = jnp.maximum(total + bias_of(2, cols), 0.0)
        for k in range(cols // LANES):
            staged[h, k, pl.ds(y, wide_m, stride=YB), :] = value[:, k * LANES : (k + 1) * LANES]
        if h > 0 and y == YB - 2:
            flush(h - 1)

    def pack(h, z):
        for k in range(cols // LANES):
            turned = staged[h, k, z * C * YB : (z + 1) * C * YB].astype(BF16).reshape(C, YB, LANES)
            packed[h, z, :, :, k * LANES : (k + 1) * LANES] = turned

    def send(h, z):
        there = out_ref.at[:, z, :, pl.ds(h * cols, cols)]
        return pltpu.make_async_copy(packed.at[h, z], there, sems.at[h, z])

    for p in range(YB // 2 + 2):
        first(p)
    def flush(h):
        for z in range(Z):
            pack(h, z)
            send(h, z).start()

    layer(m2_ref, r2_ref, g2, e2, YB + 4, 0, X, second)
    for h in range(parts):
        layer(m3_ref, r3_ref, g3, e3, YB + 2, h * cols, cols, functools.partial(third, h))

    @pl.when(own >= 0)
    def _():
        flush(parts - 1)

    for h in range(parts):
        for z in range(Z):
            send(h, z).wait()


def on_device(tiles, entry_dest, entry_tile, entry_z, entry_xb, entry_ky, entry_kx, wy_table, wx_table,
              w_first, b_first, w_second, b_second, w_third, b_third):
    bricks = lax.axis_size("gy")
    entries = entry_dest.shape[0]
    per = entries // bricks
    n_tiles, sh, sw = tiles.shape
    dest = entry_dest.T
    tile, z, xb, ky, kx = (a.reshape(1, entries) for a in (entry_tile, entry_z, entry_xb, entry_ky, entry_kx))
    hbm = pl.BlockSpec(memory_space=pl.ANY)
    vmem = pl.BlockSpec(memory_space=pltpu.VMEM)
    kys = wy_table.shape[0]
    sent = payload_rows(per)
    send = pl.pallas_call(
        functools.partial(send_kernel, per, "gy"),
        out_shape=jax.ShapeDtypeStruct((bricks * sent, sw), BF16),
        in_specs=[hbm] * 7,
        out_specs=vmem,
        scratch_shapes=[pltpu.SMEM((1, entries), jnp.int32)] * 4
        + [
            pltpu.VMEM((n_tiles * sh, sw), BF16),
            pltpu.VMEM((kys * YB, sh), BF16),
            pltpu.VMEM((wx_table.shape[0] * sw, sw), BF16),
            pltpu.VMEM((kys, YB, min(per, 16) * sh), F32),
            pltpu.VMEM((wx_table.shape[0] // 2, per * YB, sw), F32),
            pltpu.VMEM(((bricks + 2) * sent, sw), F32),
            pltpu.SMEM((bricks,), jnp.int32),
            pltpu.SemaphoreType.DMA((7,)),
        ],
        compiler_params=pltpu.CompilerParams(vmem_limit_bytes=60 * 1024 * 1024),
        name="send",
    )(dest, tile, ky, kx, tiles.reshape(n_tiles * sh, sw), wy_table.reshape(kys * YB, sh), wx_table.reshape(-1, sw))
    arrived = lax.all_to_all(send.reshape(bricks, sent, sw), "gy", split_axis=0, concat_axis=0, tiled=True)
    arrived = arrived.reshape(bricks * sent, sw)

    chunks = entries // LANES
    wide = LANES // per * sent
    rows = X // sw * CELLS
    parts = 2
    w1 = w_first.transpose(1, 2, 3, 4, 0).reshape(9, 3, C)
    w2, w3 = (w.transpose(2, 3, 4, 0, 1).reshape(27, C, C) for w in (w_second, w_third))
    place, m1, m2, r2, m3, r3, bias = pl.pallas_call(
        functools.partial(prep_kernel, per, "gy"),
        out_shape=[
            jax.ShapeDtypeStruct((chunks, rows, wide), BF16),
            jax.ShapeDtypeStruct((2 * Z * C, 64), BF16),
            jax.ShapeDtypeStruct((2, 6 * C, 8 * C), BF16),
            jax.ShapeDtypeStruct((12 * C, 8 * C), BF16),
            jax.ShapeDtypeStruct((2, 6 * C, 8 * C), BF16),
            jax.ShapeDtypeStruct((12 * C, 8 * C), BF16),
            jax.ShapeDtypeStruct((3, Z * C, LANES), F32),
        ],
        in_specs=[vmem] * 9,
        out_specs=[vmem] * 7,
        scratch_shapes=[pltpu.VMEM((LANES, LANES), F32)],
        compiler_params=pltpu.CompilerParams(vmem_limit_bytes=24 * 1024 * 1024),
        cost_estimate=pl.CostEstimate(flops=200_000_000, bytes_accessed=3_000_000, transcendentals=0),
        name="prep",
    )(dest, z, xb, w1, b_first.reshape(1, C), w2, b_second.reshape(1, C), w3, b_third.reshape(1, C))

    return pl.pallas_call(
        functools.partial(conv_kernel, "gy", bricks),
        out_shape=jax.ShapeDtypeStruct((C, Z, YB, X), BF16),
        in_specs=[vmem] * 8,
        out_specs=pl.BlockSpec(memory_space=pl.ANY),
        scratch_shapes=[
            pltpu.VMEM((2, (YB + 4) * 8 * C, X), BF16),
            pltpu.VMEM(((YB + 4) * 2 * C, X), BF16),
            pltpu.VMEM((2, (YB + 2) * 8 * C, X), BF16),
            pltpu.VMEM(((YB + 2) * 2 * C, X), BF16),
            pltpu.VMEM((parts, X // parts // LANES, Z * C * YB, LANES), F32),
            pltpu.VMEM((parts, Z, C, YB, X // parts), BF16),
            pltpu.SemaphoreType.DMA((parts, Z)),
        ],
        compiler_params=pltpu.CompilerParams(vmem_limit_bytes=40 * 1024 * 1024),
        cost_estimate=pl.CostEstimate(flops=4_000_000_000, bytes_accessed=6_000_000, transcendentals=0),
        name="convs",
    )(arrived, place, m1, m2, r2, m3, r3, bias)


def solution(mesh):
    return jax.shard_map(
        on_device,
        mesh=mesh,
        in_specs=(
            P(("groups", "gy"), None, None),
            P("groups", None),
            P("groups"),
            P("groups"),
            P("groups"),
            P("groups"),
            P("groups"),
            P(),
            P(),
            P(),
            P(),
            P(),
            P(),
            P(),
            P(),
        ),
        out_specs=P(None, "groups", "gy", None),
        check_vma=False,
    )
```

```python
import functools

import jax
import jax.numpy as jnp
from jax import lax
from jax.experimental import pallas as pl
from jax.experimental.pallas import tpu as pltpu
from jax.sharding import PartitionSpec as P

X = 512
YB = 8
Z = 4
CAP = 4
C = 32
HALO = 3
YW = YB + 2 * HALO
CELLS = YW * Z
LANES = 128
F32 = jnp.float32
BF16 = jnp.bfloat16


def payload_rows(per):
    rows = YW * CAP
    return rows if LANES // per * rows % 16 == 0 else -(-rows // 16) * 16


def iota(shape, dim):
    return lax.broadcasted_iota(jnp.int32, shape, dim)


def send_kernel(per, axis, dest_hbm, tile_hbm, ky_hbm, kx_hbm, tiles_hbm, wy_hbm, wx_hbm, out_ref,
                dest_ref, tile_ref, ky_ref, kx_ref, tiles_ref, wy_ref, wx_ref, wyt, sorted_by, placed, count, sems):
    sources = (dest_hbm, tile_hbm, ky_hbm, kx_hbm, wy_hbm, tiles_hbm, wx_hbm)
    targets = (dest_ref, tile_ref, ky_ref, kx_ref, wy_ref, tiles_ref, wx_ref)
    copies = [pltpu.make_async_copy(a, b, sems.at[n]) for n, (a, b) in enumerate(zip(sources, targets))]
    for copy in copies:
        copy.start()

    bricks = count.shape[0]
    rows = out_ref.shape[0] // bricks
    base = lax.axis_index(axis) * per
    sh = wy_ref.shape[1]
    kys, fold = wy_ref.shape[0] // YB, sorted_by.shape[0]

    def blank(k, carry):
        sorted_by[k] = jnp.zeros(sorted_by.shape[1:], F32)
        return carry

    def clear(i, carry):
        count[i] = 0
        return carry

    def blank_placed(k, carry):
        placed[pl.ds(pl.multiple_of(k * rows, 8), rows)] = jnp.zeros((rows, placed.shape[1]), F32)
        return carry

    lax.fori_loop(0, sorted_by.shape[0], blank, 0)
    lax.fori_loop(0, bricks + 2, blank_placed, 0)
    lax.fori_loop(0, count.shape[0], clear, 0)
    group = min(per, 16)
    copies[4].wait()
    spread = (iota((sh, group * sh), 0) == iota((sh, group * sh), 1) % sh).astype(F32).astype(BF16)
    wyt[...] = jnp.dot(wy_ref[...], spread, preferred_element_type=F32).reshape(kys, YB, group * sh)
    for copy in copies[:4]:
        copy.wait()
    entry_of_col = iota((YB, group * sh), 1) // sh
    vertical = [jnp.where(entry_of_col == e % group, wyt[ky_ref[0, base + e]], 0.0) for e in range(per)]
    copies[5].wait()
    for g in range(0, per, group):
        picked = [tiles_ref[pl.ds(pl.multiple_of(tile_ref[0, base + e] * sh, sh), sh)] for e in range(g, g + group)]
        weights = jnp.concatenate(vertical[g : g + group], axis=0).astype(BF16)
        samples = jnp.dot(weights, jnp.concatenate(picked, axis=0), preferred_element_type=F32)
        samples = samples.astype(BF16).astype(F32)
        for e in range(g, g + group):
            sorted_by[kx_ref[0, base + e] % fold, e * YB : (e + 1) * YB] = samples[(e - g) * YB : (e - g + 1) * YB]
    copies[6].wait()
    by_kind = jnp.concatenate([sorted_by[k].astype(BF16) for k in range(fold)], axis=1)
    sides = [wx_ref[: fold * LANES], wx_ref[fold * LANES :]]
    patches = jnp.dot(by_kind, jnp.concatenate(sides, axis=1), preferred_element_type=F32)
    for e in range(per):
        dest = dest_ref[0, base + e]
        rank = count[dest]
        count[dest] = rank + 1
        at = (dest + 1) * rows + rank
        patch = patches[e * YB : (e + 1) * YB]
        patch = jnp.where(kx_ref[0, base + e] < fold, patch[:, :LANES], patch[:, LANES:])
        placed[pl.ds(at + HALO * CAP, YB, stride=CAP)] = patch
        placed[pl.ds(at + rows, HALO, stride=CAP)] = patch[YB - HALO :]
        placed[pl.ds(at - rows + (HALO + YB) * CAP, HALO, stride=CAP)] = patch[:HALO]
    out_ref[...] = placed[rows : rows + out_ref.shape[0]].astype(BF16)


def banded(w_ref, out_ref, rest_ref):
    hole = jnp.zeros((C, C), F32)

    def tap(a, b, c):
        return w_ref[(a * 3 + b) * 3 + c].astype(F32)

    for b in range(3):
        taps = [[tap(a, b, c) for a in range(3)] for c in range(3)]
        far = [piece for p in taps for piece in (p[1], p[2])]
        near = [piece for p in taps for piece in (p[0], p[1])]
        uppers = (far + [hole, hole], near + [taps[0][2], taps[1][2]])
        lowers = (far + [taps[0][0], taps[1][0]], near + [hole, hole])
        for n, rows in enumerate((uppers, lowers)):
            block = jnp.concatenate([jnp.concatenate(row, axis=1) for row in rows], axis=0)
            out_ref[n, b * 2 * C : (b + 1) * 2 * C] = block.astype(BF16)
    for y in range(6):
        reach = [r - y + 2 for r in range(4)]
        one = [piece for b in reach for piece in (tap(2, b, 2) if 0 <= b <= 2 else hole, hole)]
        two = [piece for b in reach for piece in (hole, tap(0, b, 2) if 0 <= b <= 2 else hole)]
        block = jnp.concatenate([jnp.concatenate(one, axis=1), jnp.concatenate(two, axis=1)], axis=0)
        rest_ref[y * 2 * C : (y + 1) * 2 * C] = block.astype(BF16)


def bias_rows(b_ref):
    column = jnp.sum(
        jnp.where(iota((C, C), 0) == iota((C, C), 1), jnp.broadcast_to(b_ref[...], (C, C)), 0.0), axis=1, keepdims=True
    )
    return jnp.concatenate([jnp.broadcast_to(column, (C, LANES))] * Z, axis=0)


def prep_kernel(per, axis, dest_ref, z_ref, xb_ref, w1_ref, b1_ref, w2_ref, b2_ref, w3_ref, b3_ref,
                place_ref, m1_ref, m2_ref, r2_ref, m3_ref, r3_ref, bias_ref, taps):
    own = lax.axis_index(axis)
    banded(w2_ref, m2_ref, r2_ref)
    banded(w3_ref, m3_ref, r3_ref)
    for n, b_ref in enumerate((b1_ref, b2_ref, b3_ref)):
        bias_ref[n] = bias_rows(b_ref)
    taps[...] = jnp.zeros_like(taps)
    for ab in range(9):
        taps[ab * 4 : ab * 4 + 3, :C] = w1_ref[ab].astype(F32)
    first = jnp.transpose(taps[...])[:C].astype(BF16)
    wide1 = m1_ref.shape[1]
    t = iota((LANES, wide1), 0)
    col = iota((LANES, wide1), 1)
    t_c, t_b, t_a = t % 4, (t // 4) % 3, t // 12
    for y in range(2):
        for z in range(Z):
            z_in = z + t_a - 1
            good = (t < 36) & (t_c < 3) & (z_in >= 0) & (z_in < Z)
            pick = (good & (col == t_c * (4 * Z) + (t_b + y) * Z + z_in)).astype(F32).astype(BF16)
            at = (y * Z + z) * C
            m1_ref[at : at + C, :] = jnp.dot(first, pick, preferred_element_type=F32).astype(BF16)
    chunks, rows, wide = place_ref.shape
    earlier = (
        (iota((LANES, LANES), 0) < iota((LANES, LANES), 1))
        & (iota((LANES, LANES), 0) // per == iota((LANES, LANES), 1) // per)
    ).astype(F32).astype(BF16)
    sent = payload_rows(per)
    slot_k, y_k, src_k = iota((wide, LANES), 0) % CAP, iota((wide, LANES), 0) % sent // CAP, iota((wide, LANES), 0) // sent
    same_source = src_k == iota((wide, LANES), 1) // per
    code_row = (iota((rows, LANES), 0) // CELLS) * Z + iota((rows, LANES), 0) % Z
    same_y = iota((rows, wide), 0) % CELLS // Z == iota((rows, wide), 1) % sent // CAP

    def one(n, carry):
        at = pl.multiple_of(n * LANES, LANES)
        dest = jnp.broadcast_to(dest_ref[:, pl.ds(at, LANES)], (8, LANES))
        code = xb_ref[:, pl.ds(at, LANES)] * Z + z_ref[:, pl.ds(at, LANES)]
        sub = iota((8, LANES), 0)
        named = (dest == own - 1 + sub) & (sub < 3)
        rank = jnp.dot(named.astype(F32).astype(BF16), earlier, preferred_element_type=F32).astype(jnp.int32)
        slot = jnp.where(named, rank, -1)
        wanted = jnp.where(y_k < HALO, slot[0:1], jnp.where(y_k < HALO + YB, slot[1:2], slot[2:3]))
        held = (same_source & (slot_k == wanted) & (y_k < YW)).astype(F32).astype(BF16)
        cell = (code_row == code).astype(F32).astype(BF16)
        hits = lax.dot_general(cell, held, (((1,), (1,)), ((), ())), preferred_element_type=F32)
        place_ref[n] = jnp.where(same_y, hits, 0.0).astype(BF16)
        return carry

    if chunks <= 8:
        for n in range(chunks):
            one(n, 0)
    else:
        lax.fori_loop(0, chunks, one, 0)


def shifted(values):
    lane = iota(values.shape, 1)
    last = values.shape[1] - 1
    zero = jnp.zeros_like(values)
    return (
        jnp.where(lane == 0, zero, pltpu.roll(values, 1, 1)),
        values,
        jnp.where(lane == last, zero, pltpu.roll(values, last, 1)),
    )


def conv_kernel(axis, bricks, arrived_ref, place_ref, m1_ref, m2_ref, r2_ref, m3_ref, r3_ref, bias_ref, out_ref,
                g2, e2, g3, e3, staged, packed, sems):
    own = lax.axis_index(axis)
    above, below = (own > 0).astype(F32), (own < bricks - 1).astype(F32)
    chunks, rows, wide = place_ref.shape
    wide_m, half = Z * C, Z * C // 2

    def place(n, total):
        at = n * wide if isinstance(n, int) else pl.multiple_of(n * wide, wide)
        return total + jnp.dot(place_ref[n], arrived_ref[pl.ds(at, wide)], preferred_element_type=F32)

    total = jnp.zeros((rows, LANES), F32)
    if chunks <= 8:
        for n in range(chunks):
            total = place(n, total)
    else:
        total = lax.fori_loop(0, chunks, place, total)
    image = jnp.concatenate([total[n * CELLS : (n + 1) * CELLS] for n in range(X // LANES)], axis=1)
    moved = shifted(image.astype(BF16).astype(F32))

    def bias_of(n, cols):
        return jnp.concatenate([bias_ref[n]] * (cols // LANES), axis=1)

    def keep(g, e, row, value):
        at = 8 * C * row
        for c, v in enumerate(shifted(value.astype(BF16))):
            g[0, at + c * half : at + (c + 1) * half] = v[:half]
            g[1, at + c * half : at + (c + 1) * half] = v[half:]
            if c < 2:
                g[0, at + (6 + c) * C : at + (7 + c) * C] = v[2 * C : 3 * C]
                g[1, at + (6 + c) * C : at + (7 + c) * C] = v[C : 2 * C]
            else:
                e[row * half : row * half + C] = v[2 * C : 3 * C]
                e[row * half + C : (row + 1) * half] = v[C : 2 * C]

    def first(p):
        gathered = jnp.concatenate([m[2 * p * Z : (2 * p + 4) * Z] for m in moved], axis=0)
        gathered = jnp.concatenate([gathered, jnp.zeros((m1_ref.shape[1] - 12 * Z, X), F32)], axis=0).astype(BF16)
        acc = jnp.dot(m1_ref[...], gathered, preferred_element_type=F32)
        for y in range(2):
            value = jnp.maximum(acc[y * wide_m : (y + 1) * wide_m] + bias_of(0, X), 0.0)
            if p == 0:
                value = value * above
            if p == YB // 2 + 1:
                value = value * below
            keep(g2, e2, 2 * p + y, value)

    def layer(m_ref, r_ref, g, e, rows_in, at, cols, finish):
        sums = {y: [] for y in range(rows_in - 2)}
        there = slice(at, at + cols)

        def rest(r):
            count = min(4, rows_in - r)
            low, high = max(0, r - 2), min(rows_in - 2, r + count)
            taps = slice((low - r + 2) * half, (high - r + 2) * half)
            found = jnp.dot(r_ref[taps, : count * half], e[r * half : (r + count) * half, there], preferred_element_type=F32)
            for y in range(low, high):
                sums[y].append((C, found[(y - low) * half : (y - low + 1) * half]))

        for r in range(rows_in):
            if r % 4 == 0:
                rest(r)
            low, high = max(0, r - rows_in + 3), min(2, r)
            taps = slice(low * half, (high + 1) * half)
            window = slice(8 * C * r, 8 * C * (r + 1))
            for n in range(2):
                found = jnp.dot(m_ref[n, taps], g[n, window, there], preferred_element_type=F32)
                for b in range(low, high + 1):
                    sums[r - b].append((n * half, found[(b - low) * half : (b - low + 1) * half]))
            if r >= 2:
                pieces = []
                for z in range(Z):
                    parts_z = [v[z * C - o : z * C - o + C] for o, v in sums[r - 2] if o <= z * C < o + half]
                    pieces.append(functools.reduce(lambda p, q: p + q, parts_z))
                finish(r - 2, jnp.concatenate(pieces, axis=0))

    def second(y, total):
        value = jnp.maximum(total + bias_of(1, X), 0.0)
        if y == 0:
            value = value * above
        if y == YB + 1:
            value = value * below
        keep(g3, e3, y, value)

    parts, cols = packed.shape[0], packed.shape[4]

    def third(h, y, total):
        value = jnp.maximum(total + bias_of(2, cols), 0.0)
        for k in range(cols // LANES):
            staged[h, k, pl.ds(y, wide_m, stride=YB), :] = value[:, k * LANES : (k + 1) * LANES]
        if h > 0 and y == YB - 2:
            flush(h - 1)

    def pack(h, z):
        rows_of = slice(z * C * YB, (z + 1) * C * YB)
        turned = [staged[h, k, rows_of].reshape(C, YB, LANES) for k in range(cols // LANES)]
        packed[h, z] = jnp.concatenate(turned, axis=2).astype(BF16)

    def send(h, z):
        there = out_ref.at[:, z, :, pl.ds(h * cols, cols)]
        return pltpu.make_async_copy(packed.at[h, z], there, sems.at[h, z])

    for p in range(YB // 2 + 2):
        first(p)
    def flush(h):
        for z in range(Z):
            pack(h, z)
            send(h, z).start()

    layer(m2_ref, r2_ref, g2, e2, YB + 4, 0, X, second)
    for h in range(parts):
        layer(m3_ref, r3_ref, g3, e3, YB + 2, h * cols, cols, functools.partial(third, h))

    @pl.when(own >= 0)
    def _():
        flush(parts - 1)

    for h in range(parts):
        for z in range(Z):
            send(h, z).wait()


def on_device(tiles, entry_dest, entry_tile, entry_z, entry_xb, entry_ky, entry_kx, wy_table, wx_table,
              w_first, b_first, w_second, b_second, w_third, b_third):
    bricks = lax.axis_size("gy")
    entries = entry_dest.shape[0]
    per = entries // bricks
    n_tiles, sh, sw = tiles.shape
    dest = entry_dest.T
    tile, z, xb, ky, kx = (a.reshape(1, entries) for a in (entry_tile, entry_z, entry_xb, entry_ky, entry_kx))
    hbm = pl.BlockSpec(memory_space=pl.ANY)
    vmem = pl.BlockSpec(memory_space=pltpu.VMEM)
    kys = wy_table.shape[0]
    sent = payload_rows(per)
    send = pl.pallas_call(
        functools.partial(send_kernel, per, "gy"),
        out_shape=jax.ShapeDtypeStruct((bricks * sent, sw), BF16),
        in_specs=[hbm] * 7,
        out_specs=vmem,
        scratch_shapes=[pltpu.SMEM((1, entries), jnp.int32)] * 4
        + [
            pltpu.VMEM((n_tiles * sh, sw), BF16),
            pltpu.VMEM((kys * YB, sh), BF16),
            pltpu.VMEM((wx_table.shape[0] * sw, sw), BF16),
            pltpu.VMEM((kys, YB, min(per, 16) * sh), F32),
            pltpu.VMEM((wx_table.shape[0] // 2, per * YB, sw), F32),
            pltpu.VMEM(((bricks + 2) * sent, sw), F32),
            pltpu.SMEM((bricks,), jnp.int32),
            pltpu.SemaphoreType.DMA((7,)),
        ],
        compiler_params=pltpu.CompilerParams(vmem_limit_bytes=60 * 1024 * 1024),
        name="send",
    )(dest, tile, ky, kx, tiles.reshape(n_tiles * sh, sw), wy_table.reshape(kys * YB, sh), wx_table.reshape(-1, sw))
    arrived = lax.all_to_all(send.reshape(bricks, sent, sw), "gy", split_axis=0, concat_axis=0, tiled=True)
    arrived = arrived.reshape(bricks * sent, sw)

    chunks = entries // LANES
    wide = LANES // per * sent
    rows = X // sw * CELLS
    parts = 2
    w1 = w_first.transpose(1, 2, 3, 4, 0).reshape(9, 3, C)
    w2, w3 = (w.transpose(2, 3, 4, 0, 1).reshape(27, C, C) for w in (w_second, w_third))
    place, m1, m2, r2, m3, r3, bias = pl.pallas_call(
        functools.partial(prep_kernel, per, "gy"),
        out_shape=[
            jax.ShapeDtypeStruct((chunks, rows, wide), BF16),
            jax.ShapeDtypeStruct((2 * Z * C, 64), BF16),
            jax.ShapeDtypeStruct((2, 6 * C, 8 * C), BF16),
            jax.ShapeDtypeStruct((12 * C, 8 * C), BF16),
            jax.ShapeDtypeStruct((2, 6 * C, 8 * C), BF16),
            jax.ShapeDtypeStruct((12 * C, 8 * C), BF16),
            jax.ShapeDtypeStruct((3, Z * C, LANES), F32),
        ],
        in_specs=[vmem] * 9,
        out_specs=[vmem] * 7,
        scratch_shapes=[pltpu.VMEM((LANES, LANES), F32)],
        compiler_params=pltpu.CompilerParams(vmem_limit_bytes=24 * 1024 * 1024),
        cost_estimate=pl.CostEstimate(flops=200_000_000, bytes_accessed=3_000_000, transcendentals=0),
        name="prep",
    )(dest, z, xb, w1, b_first.reshape(1, C), w2, b_second.reshape(1, C), w3, b_third.reshape(1, C))

    return pl.pallas_call(
        functools.partial(conv_kernel, "gy", bricks),
        out_shape=jax.ShapeDtypeStruct((C, Z, YB, X), BF16),
        in_specs=[vmem] * 8,
        out_specs=pl.BlockSpec(memory_space=pl.ANY),
        scratch_shapes=[
            pltpu.VMEM((2, (YB + 4) * 8 * C, X), BF16),
            pltpu.VMEM(((YB + 4) * 2 * C, X), BF16),
            pltpu.VMEM((2, (YB + 2) * 8 * C, X), BF16),
            pltpu.VMEM(((YB + 2) * 2 * C, X), BF16),
            pltpu.VMEM((parts, X // parts // LANES, Z * C * YB, LANES), F32),
            pltpu.VMEM((parts, Z, C, YB, X // parts), BF16),
            pltpu.SemaphoreType.DMA((parts, Z)),
        ],
        compiler_params=pltpu.CompilerParams(vmem_limit_bytes=40 * 1024 * 1024),
        cost_estimate=pl.CostEstimate(flops=4_000_000_000, bytes_accessed=6_000_000, transcendentals=0),
        name="convs",
    )(arrived, place, m1, m2, r2, m3, r3, bias)


def solution(mesh):
    return jax.shard_map(
        on_device,
        mesh=mesh,
        in_specs=(
            P(("groups", "gy"), None, None),
            P("groups", None),
            P("groups"),
            P("groups"),
            P("groups"),
            P("groups"),
            P("groups"),
            P(),
            P(),
            P(),
            P(),
            P(),
            P(),
            P(),
            P(),
        ),
        out_specs=P(None, "groups", "gy", None),
        check_vma=False,
    )
```

```python
import functools

import jax
import jax.numpy as jnp
from jax import lax
from jax.experimental import pallas as pl
from jax.experimental.pallas import tpu as pltpu
from jax.sharding import PartitionSpec as P

X = 512
YB = 8
Z = 4
CAP = 4
C = 32
HALO = 3
YW = YB + 2 * HALO
CELLS = YW * Z
LANES = 128
F32 = jnp.float32
BF16 = jnp.bfloat16


def payload_rows(per):
    rows = YW * CAP
    return rows if LANES // per * rows % 16 == 0 else -(-rows // 16) * 16


def iota(shape, dim):
    return lax.broadcasted_iota(jnp.int32, shape, dim)


def send_kernel(per, axis, dest_hbm, tile_hbm, ky_hbm, kx_hbm, tiles_hbm, wy_hbm, wx_hbm, out_ref,
                dest_ref, tile_ref, ky_ref, kx_ref, tiles_ref, wy_ref, wx_ref, wyt, sorted_by, placed, count, sems):
    sources = (dest_hbm, tile_hbm, ky_hbm, kx_hbm, wy_hbm, tiles_hbm, wx_hbm)
    targets = (dest_ref, tile_ref, ky_ref, kx_ref, wy_ref, tiles_ref, wx_ref)
    copies = [pltpu.make_async_copy(a, b, sems.at[n]) for n, (a, b) in enumerate(zip(sources, targets))]
    for copy in copies:
        copy.start()

    bricks = count.shape[0]
    rows = out_ref.shape[0] // bricks
    base = lax.axis_index(axis) * per
    sh = wy_ref.shape[1]
    kys, fold = wy_ref.shape[0] // YB, sorted_by.shape[0]

    def blank(k, carry):
        sorted_by[k] = jnp.zeros(sorted_by.shape[1:], F32)
        return carry

    def clear(i, carry):
        count[i] = 0
        return carry

    def blank_placed(k, carry):
        placed[pl.ds(pl.multiple_of(k * rows, 8), rows)] = jnp.zeros((rows, placed.shape[1]), F32)
        return carry

    lax.fori_loop(0, sorted_by.shape[0], blank, 0)
    lax.fori_loop(0, bricks + 2, blank_placed, 0)
    lax.fori_loop(0, count.shape[0], clear, 0)
    group = min(per, 16)
    copies[4].wait()
    spread = (iota((sh, group * sh), 0) == iota((sh, group * sh), 1) % sh).astype(F32).astype(BF16)
    wyt[...] = jnp.dot(wy_ref[...], spread, preferred_element_type=F32).reshape(kys, YB, group * sh)
    for copy in copies[:4]:
        copy.wait()
    entry_of_col = iota((YB, group * sh), 1) // sh
    vertical = [jnp.where(entry_of_col == e % group, wyt[ky_ref[0, base + e]], 0.0) for e in range(per)]
    copies[5].wait()
    for g in range(0, per, group):
        picked = [tiles_ref[pl.ds(pl.multiple_of(tile_ref[0, base + e] * sh, sh), sh)] for e in range(g, g + group)]
        weights = jnp.concatenate(vertical[g : g + group], axis=0).astype(BF16)
        samples = jnp.dot(weights, jnp.concatenate(picked, axis=0), preferred_element_type=F32)
        samples = samples.astype(BF16).astype(F32)
        for e in range(g, g + group):
            sorted_by[kx_ref[0, base + e] % fold, e * YB : (e + 1) * YB] = samples[(e - g) * YB : (e - g + 1) * YB]
    copies[6].wait()
    by_kind = jnp.concatenate([sorted_by[k].astype(BF16) for k in range(fold)], axis=1)
    sides = [wx_ref[: fold * LANES], wx_ref[fold * LANES :]]
    patches = jnp.dot(by_kind, jnp.concatenate(sides, axis=1), preferred_element_type=F32)
    for e in range(per):
        dest = dest_ref[0, base + e]
        rank = count[dest]
        count[dest] = rank + 1
        at = (dest + 1) * rows + rank
        patch = patches[e * YB : (e + 1) * YB]
        patch = jnp.where(kx_ref[0, base + e] < fold, patch[:, :LANES], patch[:, LANES:])
        placed[pl.ds(at + HALO * CAP, YB, stride=CAP)] = patch
        placed[pl.ds(at + rows, HALO, stride=CAP)] = patch[YB - HALO :]
        placed[pl.ds(at - rows + (HALO + YB) * CAP, HALO, stride=CAP)] = patch[:HALO]
    out_ref[...] = placed[rows : rows + out_ref.shape[0]].astype(BF16)


def banded(w_ref, out_ref, rest_ref):
    hole = jnp.zeros((C, C), F32)

    def tap(a, b, c):
        return w_ref[(a * 3 + b) * 3 + c].astype(F32)

    for b in range(3):
        taps = [[tap(a, b, c) for a in range(3)] for c in range(3)]
        far = [piece for p in taps for piece in (p[1], p[2])]
        near = [piece for p in taps for piece in (p[0], p[1])]
        uppers = (far + [hole, hole], near + [taps[0][2], taps[1][2]])
        lowers = (far + [taps[0][0], taps[1][0]], near + [hole, hole])
        for n, rows in enumerate((uppers, lowers)):
            block = jnp.concatenate([jnp.concatenate(row, axis=1) for row in rows], axis=0)
            out_ref[n, b * 2 * C : (b + 1) * 2 * C] = block.astype(BF16)
    for y in range(6):
        reach = [r - y + 2 for r in range(4)]
        one = [piece for b in reach for piece in (tap(2, b, 2) if 0 <= b <= 2 else hole, hole)]
        two = [piece for b in reach for piece in (hole, tap(0, b, 2) if 0 <= b <= 2 else hole)]
        block = jnp.concatenate([jnp.concatenate(one, axis=1), jnp.concatenate(two, axis=1)], axis=0)
        rest_ref[y * 2 * C : (y + 1) * 2 * C] = block.astype(BF16)


def bias_rows(b_ref):
    column = jnp.sum(
        jnp.where(iota((C, C), 0) == iota((C, C), 1), jnp.broadcast_to(b_ref[...], (C, C)), 0.0), axis=1, keepdims=True
    )
    return jnp.concatenate([jnp.broadcast_to(column, (C, LANES))] * Z, axis=0)


def prep_kernel(per, axis, dest_ref, z_ref, xb_ref, w1_ref, b1_ref, w2_ref, b2_ref, w3_ref, b3_ref,
                place_ref, m1_ref, m2_ref, r2_ref, m3_ref, r3_ref, bias_ref, taps):
    own = lax.axis_index(axis)
    banded(w2_ref, m2_ref, r2_ref)
    banded(w3_ref, m3_ref, r3_ref)
    for n, b_ref in enumerate((b1_ref, b2_ref, b3_ref)):
        bias_ref[n] = bias_rows(b_ref)
    taps[...] = jnp.zeros_like(taps)
    for ab in range(9):
        taps[ab * 4 : ab * 4 + 3, :C] = w1_ref[ab].astype(F32)
    first = jnp.transpose(taps[...])[:C].astype(BF16)
    wide1 = m1_ref.shape[1]
    t = iota((LANES, wide1), 0)
    col = iota((LANES, wide1), 1)
    t_c, t_b, t_a = t % 4, (t // 4) % 3, t // 12
    for y in range(2):
        for z in range(Z):
            z_in = z + t_a - 1
            good = (t < 36) & (t_c < 3) & (z_in >= 0) & (z_in < Z)
            pick = (good & (col == t_c * (4 * Z) + (t_b + y) * Z + z_in)).astype(F32).astype(BF16)
            at = (y * Z + z) * C
            m1_ref[at : at + C, :] = jnp.dot(first, pick, preferred_element_type=F32).astype(BF16)
    chunks, rows, wide = place_ref.shape
    earlier = (
        (iota((LANES, LANES), 0) < iota((LANES, LANES), 1))
        & (iota((LANES, LANES), 0) // per == iota((LANES, LANES), 1) // per)
    ).astype(F32).astype(BF16)
    sent = payload_rows(per)
    slot_k, y_k, src_k = iota((wide, LANES), 0) % CAP, iota((wide, LANES), 0) % sent // CAP, iota((wide, LANES), 0) // sent
    same_source = src_k == iota((wide, LANES), 1) // per
    code_row = (iota((rows, LANES), 0) // CELLS) * Z + iota((rows, LANES), 0) % Z
    same_y = iota((rows, wide), 0) % CELLS // Z == iota((rows, wide), 1) % sent // CAP

    def one(n, carry):
        at = pl.multiple_of(n * LANES, LANES)
        dest = jnp.broadcast_to(dest_ref[:, pl.ds(at, LANES)], (8, LANES))
        code = xb_ref[:, pl.ds(at, LANES)] * Z + z_ref[:, pl.ds(at, LANES)]
        sub = iota((8, LANES), 0)
        named = (dest == own - 1 + sub) & (sub < 3)
        rank = jnp.dot(named.astype(F32).astype(BF16), earlier, preferred_element_type=F32).astype(jnp.int32)
        slot = jnp.where(named, rank, -1)
        wanted = jnp.where(y_k < HALO, slot[0:1], jnp.where(y_k < HALO + YB, slot[1:2], slot[2:3]))
        held = (same_source & (slot_k == wanted) & (y_k < YW)).astype(F32).astype(BF16)
        cell = (code_row == code).astype(F32).astype(BF16)
        hits = lax.dot_general(cell, held, (((1,), (1,)), ((), ())), preferred_element_type=F32)
        place_ref[n] = jnp.where(same_y, hits, 0.0).astype(BF16)
        return carry

    if chunks <= 8:
        for n in range(chunks):
            one(n, 0)
    else:
        lax.fori_loop(0, chunks, one, 0)


def shifted(values):
    lane = iota(values.shape, 1)
    last = values.shape[1] - 1
    zero = jnp.zeros_like(values)
    return (
        jnp.where(lane == 0, zero, pltpu.roll(values, 1, 1)),
        values,
        jnp.where(lane == last, zero, pltpu.roll(values, last, 1)),
    )


def conv_kernel(axis, bricks, arrived_ref, place_ref, m1_ref, m2_ref, r2_ref, m3_ref, r3_ref, bias_ref, out_ref,
                g2, e2, g3, e3, staged, packed, sems):
    own = lax.axis_index(axis)
    above, below = (own > 0).astype(F32), (own < bricks - 1).astype(F32)
    chunks, rows, wide = place_ref.shape
    wide_m, half = Z * C, Z * C // 2

    def place(n, total):
        at = n * wide if isinstance(n, int) else pl.multiple_of(n * wide, wide)
        return total + jnp.dot(place_ref[n], arrived_ref[pl.ds(at, wide)], preferred_element_type=F32)

    total = jnp.zeros((rows, LANES), F32)
    if chunks <= 8:
        for n in range(chunks):
            total = place(n, total)
    else:
        total = lax.fori_loop(0, chunks, place, total)
    image = jnp.concatenate([total[n * CELLS : (n + 1) * CELLS] for n in range(X // LANES)], axis=1)
    moved = shifted(image.astype(BF16).astype(F32))

    def bias_of(n, cols):
        return jnp.concatenate([bias_ref[n]] * (cols // LANES), axis=1)

    def keep(g, e, row, value):
        at = 8 * C * row
        for c, v in enumerate(shifted(value.astype(BF16))):
            g[0, at + c * half : at + (c + 1) * half] = v[:half]
            g[1, at + c * half : at + (c + 1) * half] = v[half:]
            if c < 2:
                g[0, at + (6 + c) * C : at + (7 + c) * C] = v[2 * C : 3 * C]
                g[1, at + (6 + c) * C : at + (7 + c) * C] = v[C : 2 * C]
            else:
                e[row * half : row * half + C] = v[2 * C : 3 * C]
                e[row * half + C : (row + 1) * half] = v[C : 2 * C]

    def first(p):
        gathered = jnp.concatenate([m[2 * p * Z : (2 * p + 4) * Z] for m in moved], axis=0)
        gathered = jnp.concatenate([gathered, jnp.zeros((m1_ref.shape[1] - 12 * Z, X), F32)], axis=0).astype(BF16)
        acc = jnp.dot(m1_ref[...], gathered, preferred_element_type=F32)
        for y in range(2):
            value = jnp.maximum(acc[y * wide_m : (y + 1) * wide_m] + bias_of(0, X), 0.0)
            if p == 0:
                value = value * above
            if p == YB // 2 + 1:
                value = value * below
            keep(g2, e2, 2 * p + y, value)

    def layer(m_ref, r_ref, g, e, rows_in, at, cols, finish):
        sums = {y: [] for y in range(rows_in - 2)}
        there = slice(at, at + cols)

        def rest(r):
            count = min(4, rows_in - r)
            low, high = max(0, r - 2), min(rows_in - 2, r + count)
            taps = slice((low - r + 2) * half, (high - r + 2) * half)
            found = jnp.dot(r_ref[taps, : count * half], e[r * half : (r + count) * half, there], preferred_element_type=F32)
            for y in range(low, high):
                sums[y].append((C, found[(y - low) * half : (y - low + 1) * half]))

        for r in range(rows_in):
            if r % 4 == 0:
                rest(r)
            low, high = max(0, r - rows_in + 3), min(2, r)
            taps = slice(low * half, (high + 1) * half)
            window = slice(8 * C * r, 8 * C * (r + 1))
            for n in range(2):
                found = jnp.dot(m_ref[n, taps], g[n, window, there], preferred_element_type=F32)
                for b in range(low, high + 1):
                    sums[r - b].append((n * half, found[(b - low) * half : (b - low + 1) * half]))
            if r >= 2:
                pieces = []
                for z in range(Z):
                    parts_z = [v[z * C - o : z * C - o + C] for o, v in sums[r - 2] if o <= z * C < o + half]
                    pieces.append(functools.reduce(lambda p, q: p + q, parts_z))
                finish(r - 2, jnp.concatenate(pieces, axis=0))

    def second(y, total):
        value = jnp.maximum(total + bias_of(1, X), 0.0)
        if y == 0:
            value = value * above
        if y == YB + 1:
            value = value * below
        keep(g3, e3, y, value)

    parts, cols = packed.shape[0], packed.shape[4]

    def third(h, y, total):
        value = jnp.maximum(total + bias_of(2, cols), 0.0)
        for k in range(cols // LANES):
            staged[h, k, pl.ds(y, wide_m, stride=YB), :] = value[:, k * LANES : (k + 1) * LANES]
        if h > 0 and y == YB - 2:
            flush(h - 1)

    def pack(h, z):
        rows_of = slice(z * C * YB, (z + 1) * C * YB)
        turned = [staged[h, k, rows_of].reshape(C, YB, LANES) for k in range(cols // LANES)]
        packed[h, z] = jnp.concatenate(turned, axis=2).astype(BF16)

    def send(h, z):
        there = out_ref.at[:, z, :, pl.ds(h * cols, cols)]
        return pltpu.make_async_copy(packed.at[h, z], there, sems.at[h, z])

    for p in range(YB // 2 + 2):
        first(p)
    def flush(h):
        for z in range(Z):
            pack(h, z)
            send(h, z).start()

    layer(m2_ref, r2_ref, g2, e2, YB + 4, 0, X, second)
    for h in range(parts):
        layer(m3_ref, r3_ref, g3, e3, YB + 2, h * cols, cols, functools.partial(third, h))

    @pl.when(own >= 0)
    def _():
        flush(parts - 1)

    for h in range(parts):
        for z in range(Z):
            send(h, z).wait()


def on_device(tiles, entry_dest, entry_tile, entry_z, entry_xb, entry_ky, entry_kx, wy_table, wx_table,
              w_first, b_first, w_second, b_second, w_third, b_third):
    bricks = lax.axis_size("gy")
    entries = entry_dest.shape[0]
    per = entries // bricks
    n_tiles, sh, sw = tiles.shape
    dest = entry_dest.T
    tile, z, xb, ky, kx = (a.reshape(1, entries) for a in (entry_tile, entry_z, entry_xb, entry_ky, entry_kx))
    hbm = pl.BlockSpec(memory_space=pl.ANY)
    vmem = pl.BlockSpec(memory_space=pltpu.VMEM)
    kys = wy_table.shape[0]
    sent = payload_rows(per)
    send = pl.pallas_call(
        functools.partial(send_kernel, per, "gy"),
        out_shape=jax.ShapeDtypeStruct((bricks * sent, sw), BF16),
        in_specs=[hbm] * 7,
        out_specs=vmem,
        scratch_shapes=[pltpu.SMEM((1, entries), jnp.int32)] * 4
        + [
            pltpu.VMEM((n_tiles * sh, sw), BF16),
            pltpu.VMEM((kys * YB, sh), BF16),
            pltpu.VMEM((wx_table.shape[0] * sw, sw), BF16),
            pltpu.VMEM((kys, YB, min(per, 16) * sh), F32),
            pltpu.VMEM((wx_table.shape[0] // 2, per * YB, sw), F32),
            pltpu.VMEM(((bricks + 2) * sent, sw), F32),
            pltpu.SMEM((bricks,), jnp.int32),
            pltpu.SemaphoreType.DMA((7,)),
        ],
        compiler_params=pltpu.CompilerParams(vmem_limit_bytes=60 * 1024 * 1024),
        name="send",
    )(dest, tile, ky, kx, tiles.reshape(n_tiles * sh, sw), wy_table.reshape(kys * YB, sh), wx_table.reshape(-1, sw))
    arrived = lax.all_to_all(send.reshape(bricks, sent, sw), "gy", split_axis=0, concat_axis=0, tiled=True)
    arrived = arrived.reshape(bricks * sent, sw)

    chunks = entries // LANES
    wide = LANES // per * sent
    rows = X // sw * CELLS
    parts = 2
    w1 = w_first.transpose(1, 2, 3, 4, 0).reshape(9, 3, C)
    w2, w3 = (w.transpose(2, 3, 4, 0, 1).reshape(27, C, C) for w in (w_second, w_third))
    place, m1, m2, r2, m3, r3, bias = pl.pallas_call(
        functools.partial(prep_kernel, per, "gy"),
        out_shape=[
            jax.ShapeDtypeStruct((chunks, rows, wide), BF16),
            jax.ShapeDtypeStruct((2 * Z * C, 64), BF16),
            jax.ShapeDtypeStruct((2, 6 * C, 8 * C), BF16),
            jax.ShapeDtypeStruct((12 * C, 8 * C), BF16),
            jax.ShapeDtypeStruct((2, 6 * C, 8 * C), BF16),
            jax.ShapeDtypeStruct((12 * C, 8 * C), BF16),
            jax.ShapeDtypeStruct((3, Z * C, LANES), F32),
        ],
        in_specs=[vmem] * 9,
        out_specs=[vmem] * 7,
        scratch_shapes=[pltpu.VMEM((LANES, LANES), F32)],
        compiler_params=pltpu.CompilerParams(vmem_limit_bytes=24 * 1024 * 1024),
        cost_estimate=pl.CostEstimate(flops=200_000_000, bytes_accessed=3_000_000, transcendentals=0),
        name="prep",
    )(dest, z, xb, w1, b_first.reshape(1, C), w2, b_second.reshape(1, C), w3, b_third.reshape(1, C))

    return pl.pallas_call(
        functools.partial(conv_kernel, "gy", bricks),
        out_shape=jax.ShapeDtypeStruct((C, Z, YB, X), BF16),
        in_specs=[vmem] * 8,
        out_specs=pl.BlockSpec(memory_space=pl.ANY),
        scratch_shapes=[
            pltpu.VMEM((2, (YB + 4) * 8 * C, X), BF16),
            pltpu.VMEM(((YB + 4) * 2 * C, X), BF16),
            pltpu.VMEM((2, (YB + 2) * 8 * C, X), BF16),
            pltpu.VMEM(((YB + 2) * 2 * C, X), BF16),
            pltpu.VMEM((parts, X // parts // LANES, (Z * C + 1) * YB, LANES), F32),
            pltpu.VMEM((parts, Z, C, YB, X // parts), BF16),
            pltpu.SemaphoreType.DMA((parts, Z)),
        ],
        compiler_params=pltpu.CompilerParams(vmem_limit_bytes=40 * 1024 * 1024),
        cost_estimate=pl.CostEstimate(flops=4_000_000_000, bytes_accessed=6_000_000, transcendentals=0),
        name="convs",
    )(arrived, place, m1, m2, r2, m3, r3, bias)


def solution(mesh):
    return jax.shard_map(
        on_device,
        mesh=mesh,
        in_specs=(
            P(("groups", "gy"), None, None),
            P("groups", None),
            P("groups"),
            P("groups"),
            P("groups"),
            P("groups"),
            P("groups"),
            P(),
            P(),
            P(),
            P(),
            P(),
            P(),
            P(),
            P(),
        ),
        out_specs=P(None, "groups", "gy", None),
        check_vma=False,
    )
```

```python
import functools

import jax
import jax.numpy as jnp
from jax import lax
from jax.experimental import pallas as pl
from jax.experimental.pallas import tpu as pltpu
from jax.sharding import PartitionSpec as P

X = 512
YB = 8
Z = 4
CAP = 4
C = 32
HALO = 3
YW = YB + 2 * HALO
CELLS = YW * Z
LANES = 128
F32 = jnp.float32
BF16 = jnp.bfloat16


def payload_rows(per):
    rows = YW * CAP
    return rows if LANES // per * rows % 16 == 0 else -(-rows // 16) * 16


def iota(shape, dim):
    return lax.broadcasted_iota(jnp.int32, shape, dim)


def send_kernel(per, axis, dest_hbm, tile_hbm, ky_hbm, kx_hbm, tiles_hbm, wy_hbm, wx_hbm, out_ref,
                dest_ref, tile_ref, ky_ref, kx_ref, tiles_ref, wy_ref, wx_ref, wyt, sorted_by, placed, count, sems):
    sources = (dest_hbm, tile_hbm, ky_hbm, kx_hbm, wy_hbm, tiles_hbm, wx_hbm)
    targets = (dest_ref, tile_ref, ky_ref, kx_ref, wy_ref, tiles_ref, wx_ref)
    copies = [pltpu.make_async_copy(a, b, sems.at[n]) for n, (a, b) in enumerate(zip(sources, targets))]
    for copy in copies:
        copy.start()

    bricks = count.shape[0]
    rows = out_ref.shape[0] // bricks
    base = lax.axis_index(axis) * per
    sh = wy_ref.shape[1]
    kys, fold = wy_ref.shape[0] // YB, sorted_by.shape[0]

    def blank(k, carry):
        sorted_by[k] = jnp.zeros(sorted_by.shape[1:], F32)
        return carry

    def clear(i, carry):
        count[i] = 0
        return carry

    def blank_placed(k, carry):
        placed[pl.ds(pl.multiple_of(k * rows, 8), rows)] = jnp.zeros((rows, placed.shape[1]), F32)
        return carry

    lax.fori_loop(0, sorted_by.shape[0], blank, 0)
    lax.fori_loop(0, bricks + 2, blank_placed, 0)
    lax.fori_loop(0, count.shape[0], clear, 0)
    group = min(per, 16)
    copies[4].wait()
    spread = (iota((sh, group * sh), 0) == iota((sh, group * sh), 1) % sh).astype(F32).astype(BF16)
    wyt[...] = jnp.dot(wy_ref[...], spread, preferred_element_type=F32).reshape(kys, YB, group * sh)
    for copy in copies[:4]:
        copy.wait()
    entry_of_col = iota((YB, group * sh), 1) // sh
    vertical = [jnp.where(entry_of_col == e % group, wyt[ky_ref[0, base + e]], 0.0) for e in range(per)]
    copies[5].wait()
    for g in range(0, per, group):
        picked = [tiles_ref[pl.ds(pl.multiple_of(tile_ref[0, base + e] * sh, sh), sh)] for e in range(g, g + group)]
        weights = jnp.concatenate(vertical[g : g + group], axis=0).astype(BF16)
        samples = jnp.dot(weights, jnp.concatenate(picked, axis=0), preferred_element_type=F32)
        samples = samples.astype(BF16).astype(F32)
        for e in range(g, g + group):
            sorted_by[kx_ref[0, base + e] % fold, e * YB : (e + 1) * YB] = samples[(e - g) * YB : (e - g + 1) * YB]
    copies[6].wait()
    by_kind = jnp.concatenate([sorted_by[k].astype(BF16) for k in range(fold)], axis=1)
    sides = [wx_ref[: fold * LANES], wx_ref[fold * LANES :]]
    patches = jnp.dot(by_kind, jnp.concatenate(sides, axis=1), preferred_element_type=F32)
    for e in range(per):
        dest = dest_ref[0, base + e]
        rank = count[dest]
        count[dest] = rank + 1
        at = (dest + 1) * rows + rank
        patch = patches[e * YB : (e + 1) * YB]
        patch = jnp.where(kx_ref[0, base + e] < fold, patch[:, :LANES], patch[:, LANES:])
        placed[pl.ds(at + HALO * CAP, YB, stride=CAP)] = patch
        placed[pl.ds(at + rows, HALO, stride=CAP)] = patch[YB - HALO :]
        placed[pl.ds(at - rows + (HALO + YB) * CAP, HALO, stride=CAP)] = patch[:HALO]
    out_ref[...] = placed[rows : rows + out_ref.shape[0]].astype(BF16)


def banded(w_ref, out_ref, rest_ref):
    hole = jnp.zeros((C, C), F32)

    def tap(a, b, c):
        return w_ref[(a * 3 + b) * 3 + c].astype(F32)

    for b in range(3):
        taps = [[tap(a, b, c) for a in range(3)] for c in range(3)]
        far = [piece for p in taps for piece in (p[1], p[2])]
        near = [piece for p in taps for piece in (p[0], p[1])]
        uppers = (far + [hole, hole], near + [taps[0][2], taps[1][2]])
        lowers = (far + [taps[0][0], taps[1][0]], near + [hole, hole])
        for n, rows in enumerate((uppers, lowers)):
            block = jnp.concatenate([jnp.concatenate(row, axis=1) for row in rows], axis=0)
            out_ref[n, b * 2 * C : (b + 1) * 2 * C] = block.astype(BF16)
    for y in range(6):
        reach = [r - y + 2 for r in range(4)]
        one = [piece for b in reach for piece in (tap(2, b, 2) if 0 <= b <= 2 else hole, hole)]
        two = [piece for b in reach for piece in (hole, tap(0, b, 2) if 0 <= b <= 2 else hole)]
        block = jnp.concatenate([jnp.concatenate(one, axis=1), jnp.concatenate(two, axis=1)], axis=0)
        rest_ref[y * 2 * C : (y + 1) * 2 * C] = block.astype(BF16)


def bias_rows(b_ref):
    column = jnp.sum(
        jnp.where(iota((C, C), 0) == iota((C, C), 1), jnp.broadcast_to(b_ref[...], (C, C)), 0.0), axis=1, keepdims=True
    )
    return jnp.concatenate([jnp.broadcast_to(column, (C, LANES))] * Z, axis=0)


def prep_kernel(per, axis, dest_ref, z_ref, xb_ref, w1_ref, b1_ref, w2_ref, b2_ref, w3_ref, b3_ref,
                place_ref, m1_ref, m2_ref, r2_ref, m3_ref, r3_ref, bias_ref, taps):
    own = lax.axis_index(axis)
    banded(w2_ref, m2_ref, r2_ref)
    banded(w3_ref, m3_ref, r3_ref)
    for n, b_ref in enumerate((b1_ref, b2_ref, b3_ref)):
        bias_ref[n] = bias_rows(b_ref)
    taps[...] = jnp.zeros_like(taps)
    for ab in range(9):
        taps[ab * 4 : ab * 4 + 3, :C] = w1_ref[ab].astype(F32)
    first = jnp.transpose(taps[...])[:C].astype(BF16)
    wide1 = m1_ref.shape[1]
    t = iota((LANES, wide1), 0)
    col = iota((LANES, wide1), 1)
    t_c, t_b, t_a = t % 4, (t // 4) % 3, t // 12
    for y in range(2):
        for z in range(Z):
            z_in = z + t_a - 1
            good = (t < 36) & (t_c < 3) & (z_in >= 0) & (z_in < Z)
            pick = (good & (col == t_c * (4 * Z) + (t_b + y) * Z + z_in)).astype(F32).astype(BF16)
            at = (y * Z + z) * C
            m1_ref[at : at + C, :] = jnp.dot(first, pick, preferred_element_type=F32).astype(BF16)
    chunks, rows, wide = place_ref.shape
    earlier = (
        (iota((LANES, LANES), 0) < iota((LANES, LANES), 1))
        & (iota((LANES, LANES), 0) // per == iota((LANES, LANES), 1) // per)
    ).astype(F32).astype(BF16)
    sent = payload_rows(per)
    slot_k, y_k, src_k = iota((wide, LANES), 0) % CAP, iota((wide, LANES), 0) % sent // CAP, iota((wide, LANES), 0) // sent
    same_source = src_k == iota((wide, LANES), 1) // per
    code_row = (iota((rows, LANES), 0) // CELLS) * Z + iota((rows, LANES), 0) % Z
    same_y = iota((rows, wide), 0) % CELLS // Z == iota((rows, wide), 1) % sent // CAP

    def one(n, carry):
        at = pl.multiple_of(n * LANES, LANES)
        dest = jnp.broadcast_to(dest_ref[:, pl.ds(at, LANES)], (8, LANES))
        code = xb_ref[:, pl.ds(at, LANES)] * Z + z_ref[:, pl.ds(at, LANES)]
        sub = iota((8, LANES), 0)
        named = (dest == own - 1 + sub) & (sub < 3)
        rank = jnp.dot(named.astype(F32).astype(BF16), earlier, preferred_element_type=F32).astype(jnp.int32)
        slot = jnp.where(named, rank, -1)
        wanted = jnp.where(y_k < HALO, slot[0:1], jnp.where(y_k < HALO + YB, slot[1:2], slot[2:3]))
        held = (same_source & (slot_k == wanted) & (y_k < YW)).astype(F32).astype(BF16)
        cell = (code_row == code).astype(F32).astype(BF16)
        hits = lax.dot_general(cell, held, (((1,), (1,)), ((), ())), preferred_element_type=F32)
        place_ref[n] = jnp.where(same_y, hits, 0.0).astype(BF16)
        return carry

    if chunks <= 8:
        for n in range(chunks):
            one(n, 0)
    else:
        lax.fori_loop(0, chunks, one, 0)


def shifted(values):
    lane = iota(values.shape, 1)
    last = values.shape[1] - 1
    zero = jnp.zeros_like(values)
    return (
        jnp.where(lane == 0, zero, pltpu.roll(values, 1, 1)),
        values,
        jnp.where(lane == last, zero, pltpu.roll(values, last, 1)),
    )


def conv_kernel(axis, bricks, arrived_ref, place_ref, m1_ref, m2_ref, r2_ref, m3_ref, r3_ref, bias_ref, out_ref,
                g2, e2, g3, e3, staged, packed, sems):
    own = lax.axis_index(axis)
    above, below = (own > 0).astype(F32), (own < bricks - 1).astype(F32)
    chunks, rows, wide = place_ref.shape
    wide_m, half = Z * C, Z * C // 2

    def place(n, total):
        at = n * wide if isinstance(n, int) else pl.multiple_of(n * wide, wide)
        return total + jnp.dot(place_ref[n], arrived_ref[pl.ds(at, wide)], preferred_element_type=F32)

    total = jnp.zeros((rows, LANES), F32)
    if chunks <= 8:
        for n in range(chunks):
            total = place(n, total)
    else:
        total = lax.fori_loop(0, chunks, place, total)
    image = jnp.concatenate([total[n * CELLS : (n + 1) * CELLS] for n in range(X // LANES)], axis=1)
    moved = shifted(image.astype(BF16).astype(F32))

    def bias_of(n, cols):
        return jnp.concatenate([bias_ref[n]] * (cols // LANES), axis=1)

    def keep(g, e, row, value):
        at = 8 * C * row
        for c, v in enumerate(shifted(value.astype(BF16))):
            g[0, at + c * half : at + (c + 1) * half] = v[:half]
            g[1, at + c * half : at + (c + 1) * half] = v[half:]
            if c < 2:
                g[0, at + (6 + c) * C : at + (7 + c) * C] = v[2 * C : 3 * C]
                g[1, at + (6 + c) * C : at + (7 + c) * C] = v[C : 2 * C]
            else:
                e[row * half : row * half + C] = v[2 * C : 3 * C]
                e[row * half + C : (row + 1) * half] = v[C : 2 * C]

    def first(p):
        gathered = jnp.concatenate([m[2 * p * Z : (2 * p + 4) * Z] for m in moved], axis=0)
        gathered = jnp.concatenate([gathered, jnp.zeros((m1_ref.shape[1] - 12 * Z, X), F32)], axis=0).astype(BF16)
        acc = jnp.dot(m1_ref[...], gathered, preferred_element_type=F32)
        for y in range(2):
            value = jnp.maximum(acc[y * wide_m : (y + 1) * wide_m] + bias_of(0, X), 0.0)
            if p == 0:
                value = value * above
            if p == YB // 2 + 1:
                value = value * below
            keep(g2, e2, 2 * p + y, value)

    def layer(m_ref, r_ref, g, e, rows_in, at, cols, finish):
        sums = {y: [] for y in range(rows_in - 2)}
        there = slice(at, at + cols)

        def rest(r):
            count = min(4, rows_in - r)
            low, high = max(0, r - 2), min(rows_in - 2, r + count)
            taps = slice((low - r + 2) * half, (high - r + 2) * half)
            found = jnp.dot(r_ref[taps, : count * half], e[r * half : (r + count) * half, there], preferred_element_type=F32)
            for y in range(low, high):
                sums[y].append((C, found[(y - low) * half : (y - low + 1) * half]))

        for r in range(rows_in):
            if r % 4 == 0:
                rest(r)
            low, high = max(0, r - rows_in + 3), min(2, r)
            taps = slice(low * half, (high + 1) * half)
            window = slice(8 * C * r, 8 * C * (r + 1))
            for n in range(2):
                found = jnp.dot(m_ref[n, taps], g[n, window, there], preferred_element_type=F32)
                for b in range(low, high + 1):
                    sums[r - b].append((n * half, found[(b - low) * half : (b - low + 1) * half]))
            if r >= 2:
                pieces = []
                for z in range(Z):
                    parts_z = [v[z * C - o : z * C - o + C] for o, v in sums[r - 2] if o <= z * C < o + half]
                    pieces.append(functools.reduce(lambda p, q: p + q, parts_z))
                finish(r - 2, jnp.concatenate(pieces, axis=0))

    def second(y, total):
        value = jnp.maximum(total + bias_of(1, X), 0.0)
        if y == 0:
            value = value * above
        if y == YB + 1:
            value = value * below
        keep(g3, e3, y, value)

    parts, cols = packed.shape[0], packed.shape[4]

    def third(h, y, total):
        value = jnp.maximum(total + bias_of(2, cols), 0.0)
        for k in range(cols // LANES):
            staged[h, k, pl.ds(y, wide_m, stride=YB), :] = value[:, k * LANES : (k + 1) * LANES]
        if h > 0 and y == YB - 1:
            flush(h - 1)

    def pack(h, z):
        rows_of = slice(z * C * YB, (z + 1) * C * YB)
        turned = [staged[h, k, rows_of].reshape(C, YB, LANES) for k in range(cols // LANES)]
        packed[h, z] = jnp.concatenate(turned, axis=2).astype(BF16)

    def send(h, z):
        there = out_ref.at[:, z, :, pl.ds(h * cols, cols)]
        return pltpu.make_async_copy(packed.at[h, z], there, sems.at[h, z])

    for p in range(YB // 2 + 2):
        first(p)
    def flush(h):
        for z in range(Z):
            pack(h, z)
            send(h, z).start()

    layer(m2_ref, r2_ref, g2, e2, YB + 4, 0, X, second)
    for h in range(parts):
        layer(m3_ref, r3_ref, g3, e3, YB + 2, h * cols, cols, functools.partial(third, h))

    @pl.when(own >= 0)
    def _():
        flush(parts - 1)

    for h in range(parts):
        for z in range(Z):
            send(h, z).wait()


def on_device(tiles, entry_dest, entry_tile, entry_z, entry_xb, entry_ky, entry_kx, wy_table, wx_table,
              w_first, b_first, w_second, b_second, w_third, b_third):
    bricks = lax.axis_size("gy")
    entries = entry_dest.shape[0]
    per = entries // bricks
    n_tiles, sh, sw = tiles.shape
    dest = entry_dest.T
    tile, z, xb, ky, kx = (a.reshape(1, entries) for a in (entry_tile, entry_z, entry_xb, entry_ky, entry_kx))
    hbm = pl.BlockSpec(memory_space=pl.ANY)
    vmem = pl.BlockSpec(memory_space=pltpu.VMEM)
    kys = wy_table.shape[0]
    sent = payload_rows(per)
    send = pl.pallas_call(
        functools.partial(send_kernel, per, "gy"),
        out_shape=jax.ShapeDtypeStruct((bricks * sent, sw), BF16),
        in_specs=[hbm] * 7,
        out_specs=vmem,
        scratch_shapes=[pltpu.SMEM((1, entries), jnp.int32)] * 4
        + [
            pltpu.VMEM((n_tiles * sh, sw), BF16),
            pltpu.VMEM((kys * YB, sh), BF16),
            pltpu.VMEM((wx_table.shape[0] * sw, sw), BF16),
            pltpu.VMEM((kys, YB, min(per, 16) * sh), F32),
            pltpu.VMEM((wx_table.shape[0] // 2, per * YB, sw), F32),
            pltpu.VMEM(((bricks + 2) * sent, sw), F32),
            pltpu.SMEM((bricks,), jnp.int32),
            pltpu.SemaphoreType.DMA((7,)),
        ],
        compiler_params=pltpu.CompilerParams(vmem_limit_bytes=60 * 1024 * 1024),
        name="send",
    )(dest, tile, ky, kx, tiles.reshape(n_tiles * sh, sw), wy_table.reshape(kys * YB, sh), wx_table.reshape(-1, sw))
    arrived = lax.all_to_all(send.reshape(bricks, sent, sw), "gy", split_axis=0, concat_axis=0, tiled=True)
    arrived = arrived.reshape(bricks * sent, sw)

    chunks = entries // LANES
    wide = LANES // per * sent
    rows = X // sw * CELLS
    parts = 2
    w1 = w_first.transpose(1, 2, 3, 4, 0).reshape(9, 3, C)
    w2, w3 = (w.transpose(2, 3, 4, 0, 1).reshape(27, C, C) for w in (w_second, w_third))
    place, m1, m2, r2, m3, r3, bias = pl.pallas_call(
        functools.partial(prep_kernel, per, "gy"),
        out_shape=[
            jax.ShapeDtypeStruct((chunks, rows, wide), BF16),
            jax.ShapeDtypeStruct((2 * Z * C, 64), BF16),
            jax.ShapeDtypeStruct((2, 6 * C, 8 * C), BF16),
            jax.ShapeDtypeStruct((12 * C, 8 * C), BF16),
            jax.ShapeDtypeStruct((2, 6 * C, 8 * C), BF16),
            jax.ShapeDtypeStruct((12 * C, 8 * C), BF16),
            jax.ShapeDtypeStruct((3, Z * C, LANES), F32),
        ],
        in_specs=[vmem] * 9,
        out_specs=[vmem] * 7,
        scratch_shapes=[pltpu.VMEM((LANES, LANES), F32)],
        compiler_params=pltpu.CompilerParams(vmem_limit_bytes=24 * 1024 * 1024),
        cost_estimate=pl.CostEstimate(flops=200_000_000, bytes_accessed=3_000_000, transcendentals=0),
        name="prep",
    )(dest, z, xb, w1, b_first.reshape(1, C), w2, b_second.reshape(1, C), w3, b_third.reshape(1, C))

    return pl.pallas_call(
        functools.partial(conv_kernel, "gy", bricks),
        out_shape=jax.ShapeDtypeStruct((C, Z, YB, X), BF16),
        in_specs=[vmem] * 8,
        out_specs=pl.BlockSpec(memory_space=pl.ANY),
        scratch_shapes=[
            pltpu.VMEM((2, (YB + 4) * 8 * C, X), BF16),
            pltpu.VMEM(((YB + 4) * 2 * C, X), BF16),
            pltpu.VMEM((2, (YB + 2) * 8 * C, X), BF16),
            pltpu.VMEM(((YB + 2) * 2 * C, X), BF16),
            pltpu.VMEM((parts, X // parts // LANES, (Z * C + 1) * YB, LANES), F32),
            pltpu.VMEM((parts, Z, C, YB, X // parts), BF16),
            pltpu.SemaphoreType.DMA((parts, Z)),
        ],
        compiler_params=pltpu.CompilerParams(vmem_limit_bytes=40 * 1024 * 1024),
        cost_estimate=pl.CostEstimate(flops=4_000_000_000, bytes_accessed=6_000_000, transcendentals=0),
        name="convs",
    )(arrived, place, m1, m2, r2, m3, r3, bias)


def solution(mesh):
    return jax.shard_map(
        on_device,
        mesh=mesh,
        in_specs=(
            P(("groups", "gy"), None, None),
            P("groups", None),
            P("groups"),
            P("groups"),
            P("groups"),
            P("groups"),
            P("groups"),
            P(),
            P(),
            P(),
            P(),
            P(),
            P(),
            P(),
            P(),
        ),
        out_specs=P(None, "groups", "gy", None),
        check_vma=False,
    )
```
